32 devices in a mesh: groups: 2 (over x), dp: 8 (over z, y), tensor: 2 (over core).
Axes of the slice: x: 2, y: 2, z: 4, core: 2. Of those that a mesh axis runs over, the one named last changes fastest.
Arguments:
- tokens: bfloat16 [12288, 8192], P(('groups', 'dp'), 'tensor'), parts along dimension 0, may hold values from -6 to 6
- key_projection_weight: bfloat16 [8192, 1024], P('tensor'), may hold values from -0.0625 to 0.0625
- adapter_down_weight: bfloat16 [8, 64, 8192], P('dp', None, 'tensor'), may hold values from -0.0625 to 0.0625
- adapter_up_weight: bfloat16 [8, 64, 1024], P('dp', None, 'tensor'), may hold values from -0.75 to 0.75
- adapter_pool_index: int32 [8], replicated, may hold values from 0 to 7, each once
- block_adapter_index: int32 [96, 1], P('groups'), parts along dimension 0, may hold values from 0 to 7
- block_live_tokens: int32 [96], P('groups'), parts along dimension 0, may hold values from 1 to 128
Outputs:
- keys: bfloat16 [12288, 1024], P(('groups', 'dp'), 'tensor'), parts along dimension 0
The draws below stay inside these ranges and needn't reach their ends.
There are 2 independent parts, one for each index of `groups`. The reference program is written for one: setup_inputs(seed, part) draws one part's arguments, and reference() takes and returns one part's arrays. A program takes and returns all parts, laid end to end along the dimension named above; an argument that names none is the same for every part. Nothing has to cross between parts.
Inputs may be any that keep to these rules, and one draw needn't show every extreme that they name: `block_adapter_index`: every adapter is named by some block. `adapter_pool_index`: a permutation of the pool indices.
All inputs are finite; a program needn't handle non-finite values.
Results may differ from the reference program's by a relative error of at most 0.001.
Values may be sent and summed in bfloat16 or wider, within the bound.
No kernel may reach another device: no remote copies, remote signals or barrier semaphores. Data moves between devices by JAX's collectives and lax.ppermute only.
A program may use at most 128 MiB of HBM per device.

```python
import jax
import jax.numpy as jnp
from jax import lax

MODEL_WIDTH = 8192
KEY_FEATURES = 1024
ADAPTER_RANK = 64
BLK = 128
TOKEN_TOTAL = 6144
BLOCKS = 48
ADAPTER_COUNT = 8


def draw_block_live_tokens(key, part):
    key = jax.random.fold_in(key, 11)
    first_key, second_key, third_key = jax.random.split(key, 3)
    fill_values = jax.random.randint(first_key, (BLOCKS,), 1, BLK + 1)
    first_spot = jax.random.randint(second_key, (), 0, BLOCKS)
    second_spot = (first_spot + 1 + jax.random.randint(third_key, (), 0, BLOCKS - 1)) % BLOCKS
    fill_values = fill_values.at[first_spot].set(BLK)
    fill_values = fill_values.at[second_spot].set(1)
    return fill_values.astype(jnp.int32)


def steps_of(stream_key, extent, cuts, least, top_value):
    level, own = 1.0, jax.random.fold_in(stream_key, 6)
    for axis_at, parts in cuts:
        draws = jnp.exp(jax.random.uniform(jax.random.fold_in(own, axis_at), (parts,), jnp.float32, least / len(cuts), top_value / len(cuts)))
        level = level * jnp.repeat(draws, extent[axis_at] // parts).reshape([-1 if axis == axis_at else 1 for axis in range(len(extent))])
    return level


def choose_distinct(rng, rows, number_of, top, lift):
    ranking = jax.random.permutation(jax.random.fold_in(rng, 1), number_of)
    pull = ranking
    for power in range(3):
        pull = pull * pull // number_of
    pull = pull * lift // number_of
    tickets = jax.random.randint(jax.random.fold_in(rng, 2), (rows, number_of), 0, 4096) + pull
    fixed_rows = jax.random.permutation(jax.random.fold_in(rng, 3), rows)[jnp.arange(number_of) % rows]
    tickets = jnp.where(jnp.arange(rows)[:, None] == fixed_rows[None, :], 1 << 14, tickets)
    score = tickets * number_of + jnp.arange(number_of)
    return lax.top_k(score.astype(jnp.int32), top)[1].astype(jnp.int32)


def gaussian(key, shape, deviation, limit, pieces=(), kind=jnp.bfloat16):
    entries = jax.random.normal(key, shape, jnp.float32) * deviation
    if len(pieces) > 0:
        entries = steps_of(key, shape, pieces, -0.22, 0.18) * entries
    return jnp.clip(entries, min=-limit, max=limit).astype(kind)


def setup_inputs(seed: int = 0, part: int = 0) -> dict:
    keys = jax.random.split(jax.random.key(seed), 8)
    part_splits = jax.random.split(jax.random.fold_in(keys[7], part), 8)
    tokens = gaussian(part_splits[0], (TOKEN_TOTAL, MODEL_WIDTH), 1.0, 6.0, ((0, 8), (1, 2)))
    key_projection_weight = gaussian(keys[1], (MODEL_WIDTH, KEY_FEATURES), MODEL_WIDTH ** -0.5, 0.0625, ((0, 2),))
    adapter_down_weight = gaussian(keys[2], (ADAPTER_COUNT, ADAPTER_RANK, MODEL_WIDTH), MODEL_WIDTH ** -0.5, 0.0625, ((0, 8), (2, 2)))
    adapter_up_weight = gaussian(keys[3], (ADAPTER_COUNT, ADAPTER_RANK, KEY_FEATURES), ADAPTER_RANK ** -0.5, 0.75, ((0, 8), (2, 2)))
    adapter_pool_index = jax.random.permutation(keys[4], ADAPTER_COUNT).astype(jnp.int32)
    block_adapter_index = choose_distinct(part_splits[5], BLOCKS, ADAPTER_COUNT, 1, 2048)
    block_live_tokens = draw_block_live_tokens(jax.random.fold_in(jax.random.fold_in(keys[7], part), 71), part)
    return dict(tokens=tokens, key_projection_weight=key_projection_weight, adapter_down_weight=adapter_down_weight, adapter_up_weight=adapter_up_weight, adapter_pool_index=adapter_pool_index, block_adapter_index=block_adapter_index, block_live_tokens=block_live_tokens)


def reference(tokens, key_projection_weight, adapter_down_weight, adapter_up_weight, adapter_pool_index, block_adapter_index, block_live_tokens):
    base_output = jnp.dot(tokens, key_projection_weight, preferred_element_type=jnp.float32)
    block_pool_index = adapter_pool_index[block_adapter_index[:, 0]].astype(jnp.int32)
    token_block_list = tokens.reshape(BLOCKS, BLK, MODEL_WIDTH)

    def single_token_block(pair):
        block_rows, pool_slot_index = pair
        down_matrix = adapter_down_weight[pool_slot_index]
        up_matrix = adapter_up_weight[pool_slot_index].astype(jnp.float32)
        shrink = jnp.dot(block_rows, down_matrix.T, preferred_element_type=jnp.float32)
        return jnp.dot(shrink, up_matrix, precision=lax.Precision.HIGHEST, preferred_element_type=jnp.float32)

    adapter_output_delta = lax.map(single_token_block, (token_block_list, block_pool_index)).reshape(TOKEN_TOTAL, KEY_FEATURES)
    live_row_mask = jnp.arange(BLK, dtype=jnp.int32)[None, :] < block_live_tokens[:, None]
    live_row_mask = live_row_mask.reshape(TOKEN_TOTAL, 1)
    return jnp.where(live_row_mask, base_output + adapter_output_delta, 0.0).astype(jnp.bfloat16)
```

```python
import functools

import jax
import jax.numpy as jnp
from jax import lax
from jax.experimental import pallas as pl
from jax.experimental.pallas import tpu as pltpu
from jax.sharding import PartitionSpec as P

ADAPTER_RANK = 64
BLK = 128
VMEM_LIMIT = 48 * 1024 * 1024
SWAP = [(0, 1), (1, 0)]
NT = (((1,), (1,)), ((), ()))
TN = (((0,), (0,)), ((), ()))


def params():
    return pltpu.CompilerParams(
        dimension_semantics=("arbitrary",), vmem_limit_bytes=VMEM_LIMIT
    )


def base_kernel(place, tokens_ref, weight_ref, out_ref):
    @pl.when(pl.program_id(0) == 0)
    def _():
        out_ref[...] = jnp.zeros_like(out_ref)

    out_ref[...] += jnp.dot(
        tokens_ref[...], weight_ref[...], preferred_element_type=jnp.float32
    )


def base_half(place, tokens, weight, other):
    rows, width = tokens.shape
    half = weight.shape[1] // 2
    depth = 1024
    return pl.pallas_call(
        base_kernel,
        grid_spec=pltpu.PrefetchScalarGridSpec(
            num_scalar_prefetch=1,
            grid=(width // depth,),
            in_specs=[
                pl.BlockSpec((rows, depth), lambda k, place: (0, k)),
                pl.BlockSpec(
                    (depth, half), lambda k, place: (k, 1 - place[2] if other else place[2])
                ),
            ],
            out_specs=pl.BlockSpec((rows, half), lambda k, place: (0, 0)),
        ),
        out_shape=jax.ShapeDtypeStruct((rows, half), jnp.float32),
        compiler_params=params(),
        cost_estimate=pl.CostEstimate(
            flops=2 * rows * width * half,
            bytes_accessed=2 * rows * width + 2 * width * half + 4 * rows * half,
            transcendentals=0,
        ),
    )(place, tokens, weight)


def own_slot(place, pool_index, adapter_index):
    blocks = pl.num_programs(0)
    return pool_index[adapter_index[place[1] * blocks + pl.program_id(0)]]


def pool_of(place, step, other):
    depth = place[1] // 2
    column = place[1] - 2 * depth
    level = lax.rem(depth + 4 - step, 4)
    return 2 * level + (1 - column if other else column)


def half_of(place, kind):
    return {"a": 0, "b": 1, "own": place[0], "far": 1 - place[0]}[kind]


def shrink_kernel(pieces, has_prior, place, pool_index, adapter_index, tokens_ref, *refs):
    piece_refs, out_ref = refs[: len(pieces)], refs[-1]
    width = tokens_ref.shape[1] // 2
    slot = own_slot(place, pool_index, adapter_index)
    out_ref[...] = refs[-2][...] if has_prior else jnp.zeros_like(out_ref)
    for (step, other, kind), piece_ref in zip(pieces, piece_refs):

        @pl.when(slot == pool_of(place, step, other))
        def _(kind=kind, piece_ref=piece_ref):
            start = pl.multiple_of(half_of(place, kind) * width, width)
            out_ref[...] += lax.dot_general(
                piece_ref[:, :width],
                tokens_ref[:, pl.ds(start, width)],
                NT,
                preferred_element_type=jnp.float32,
            )


def shrink_sums(scalars, tokens, pieces, prior=None):
    rows, width = tokens.shape
    blocks = rows // BLK
    rank = ADAPTER_RANK
    block = pl.BlockSpec((rank, BLK), lambda b, *_: (0, b))
    specs = [
        pl.BlockSpec((rank, wide), functools.partial(lambda at, b, *_: (0, at), at))
        for _, at, wide, _ in pieces
    ]
    has_prior = prior is not None
    return pl.pallas_call(
        functools.partial(shrink_kernel, [name for name, *_ in pieces], has_prior),
        grid_spec=pltpu.PrefetchScalarGridSpec(
            num_scalar_prefetch=len(scalars),
            grid=(blocks,),
            in_specs=[pl.BlockSpec((BLK, width), lambda b, *_: (b, 0))]
            + specs
            + ([block] if has_prior else []),
            out_specs=block,
        ),
        out_shape=jax.ShapeDtypeStruct((rank, rows), jnp.float32),
        compiler_params=params(),
        cost_estimate=pl.CostEstimate(
            flops=8 * rows * width * rank,
            bytes_accessed=2 * rows * width + len(pieces) * rank * width,
            transcendentals=0,
        ),
    )(*scalars, tokens, *[piece[-1] for piece in pieces], *([prior] if has_prior else []))


def final_kernel(
    pieces, place, pool_index, adapter_index, live, mine_ref, far_ref, sum_ref, far_sum_ref, *refs
):
    piece_refs, out_ref, up_ref = refs[: len(pieces)], refs[-2], refs[-1]
    rank, half = piece_refs[0].shape
    slot = own_slot(place, pool_index, adapter_index)
    for (step, other, kind), piece_ref in zip(pieces, piece_refs):

        @pl.when(slot == pool_of(place, step, other))
        def _(kind=kind, piece_ref=piece_ref):
            start = pl.multiple_of(half_of(place, kind) * half, half)
            for part in range(3):
                up_ref[part * rank : (part + 1) * rank, pl.ds(start, half)] = piece_ref[...]

    total = sum_ref[...] + far_sum_ref[...]
    high = total.astype(jnp.bfloat16)
    rest = total - high.astype(jnp.float32)
    middle = rest.astype(jnp.bfloat16)
    low = (rest - middle.astype(jnp.float32)).astype(jnp.bfloat16)
    delta = lax.dot_general(
        jnp.concatenate([high, middle, low], axis=0),
        up_ref[...],
        TN,
        preferred_element_type=jnp.float32,
    )
    blocks = pl.num_programs(0)
    fill = live[place[1] * blocks + pl.program_id(0)]
    row = lax.broadcasted_iota(jnp.int32, out_ref.shape, 0)
    keys = mine_ref[...] + far_ref[...] + delta
    out_ref[...] = jnp.where(row < fill, keys, 0.0).astype(out_ref.dtype)


def final_keys(scalars, mine, far, sums, far_sums, pieces):
    rows, half = mine.shape
    rank = ADAPTER_RANK
    tile = pl.BlockSpec((BLK, half), lambda b, *_: (b, 0))
    block = pl.BlockSpec((rank, BLK), lambda b, *_: (0, b))
    specs = [
        pl.BlockSpec((rank, half // 2), functools.partial(lambda at, b, *_: (0, at), at))
        for _, at, _ in pieces
    ]
    return pl.pallas_call(
        functools.partial(final_kernel, [name for name, _, _ in pieces]),
        grid_spec=pltpu.PrefetchScalarGridSpec(
            num_scalar_prefetch=len(scalars),
            grid=(rows // BLK,),
            in_specs=[tile, tile, block, block] + specs,
            out_specs=tile,
            scratch_shapes=[pltpu.VMEM((3 * rank, half), jnp.bfloat16)],
        ),
        out_shape=jax.ShapeDtypeStruct((rows, half), jnp.bfloat16),
        compiler_params=params(),
        cost_estimate=pl.CostEstimate(
            flops=6 * rows * half * rank, bytes_accessed=10 * rows * half, transcendentals=0
        ),
    )(*scalars, mine, far, sums, far_sums, *[array for _, _, array in pieces])


def per_device_planes(
    tokens,
    key_projection_weight,
    adapter_down_weight,
    adapter_up_weight,
    adapter_pool_index,
    block_adapter_index,
    block_live_tokens,
):
    place = jnp.stack(
        [lax.axis_index("groups"), lax.axis_index("dp"), lax.axis_index("tensor")]
    ).astype(jnp.int32)
    down, up = adapter_down_weight[0], adapter_up_weight[0]
    width, half = down.shape[1] // 2, up.shape[1] // 2
    piece = width + half
    own = jnp.concatenate([down[:, :width], up[:, :half], down[:, width:], up[:, half:]], axis=1)
    first = lax.axis_index("groups") == 0
    own_half = jnp.where(first, own[:, :piece], own[:, piece:])

    def ring(array, step):
        pairs = [(2 * z + y, 2 * ((z + step) % 4) + y) for z in range(4) for y in range(2)]
        return lax.ppermute(array, "dp", pairs)

    def over_y(array):
        return lax.ppermute(array, "dp", [(i, i ^ 1) for i in range(8)])

    def over_x(array):
        return lax.ppermute(array, "groups", SWAP)

    def over_cores(array):
        return lax.ppermute(array, "tensor", SWAP)

    z1 = ring(own_half, 1)
    y0 = over_y(own)
    z3 = ring(own_half, -1)
    x1 = over_x(z1)
    y1 = over_y(z1)
    z2a = ring(z1, 1)
    x3 = over_x(z3)
    y3 = over_y(z3)
    z2b = ring(x1, 1)
    y2a = over_y(z2a)
    x1y = over_x(y1)
    x3y = over_x(y3)
    y2b = over_y(z2b)

    early = [
        ((0, False, "a"), 0, width, down),
        ((0, False, "b"), 1, width, down),
        ((0, True, "a"), 0, piece, y0),
        ((0, True, "b"), 1, piece, y0),
        ((1, False, "own"), 0, piece, z1),
        ((1, False, "far"), 0, piece, x1),
        ((3, False, "own"), 0, piece, z3),
        ((3, False, "far"), 0, piece, x3),
        ((2, False, "own"), 0, piece, z2a),
        ((1, True, "own"), 0, piece, y1),
        ((3, True, "own"), 0, piece, y3),
    ]
    late = [
        ((2, False, "far"), 0, piece, z2b),
        ((1, True, "far"), 0, piece, x1y),
        ((3, True, "far"), 0, piece, x3y),
        ((2, True, "own"), 0, piece, y2a),
        ((2, True, "far"), 0, piece, y2b),
    ]
    at_up = width // half
    ups = [
        ((0, False, "a"), 0, up),
        ((0, False, "b"), 1, up),
        ((0, True, "a"), at_up, y0),
        ((0, True, "b"), 2 * at_up + 1, y0),
    ] + [(name, at_up, array) for name, _, _, array in (early + late)[4:]]

    adapter_index = block_adapter_index[:, 0]
    scalars = (place, adapter_pool_index, adapter_index)
    base_far = over_cores(base_half(place, tokens, key_projection_weight, True))
    base_mine = base_half(place, tokens, key_projection_weight, False)
    sums = shrink_sums(scalars, tokens, early)
    sums = shrink_sums(scalars, tokens, late, sums)
    far_sums = over_cores(sums)
    return final_keys(
        (*scalars, block_live_tokens), base_mine, base_far, sums, far_sums, ups
    )


def per_device_gathered(
    tokens,
    key_projection_weight,
    adapter_down_weight,
    adapter_up_weight,
    adapter_pool_index,
    block_adapter_index,
    block_live_tokens,
):
    rows = tokens.shape[0]
    blocks = rows // BLK
    first_block = lax.axis_index("dp") * blocks
    slots = lax.dynamic_slice_in_dim(
        adapter_pool_index[block_adapter_index[:, 0]], first_block, blocks
    )
    fill = lax.dynamic_slice_in_dim(block_live_tokens, first_block, blocks)
    base_part = jnp.dot(tokens, key_projection_weight, preferred_element_type=jnp.float32)
    down = lax.all_gather(adapter_down_weight, "dp", axis=0, tiled=True)
    up = lax.all_gather(adapter_up_weight, "dp", axis=0, tiled=True)
    token_blocks = tokens.reshape(blocks, BLK, tokens.shape[1])
    shrink = jnp.einsum(
        "nrd,nbd->rnb",
        jnp.take(down, slots, axis=0),
        token_blocks,
        preferred_element_type=jnp.float32,
    )
    shrink = lax.psum(shrink.reshape(ADAPTER_RANK, rows), "tensor")
    delta = jnp.einsum(
        "rnb,nrc->nbc",
        shrink.reshape(ADAPTER_RANK, blocks, BLK),
        jnp.take(up, slots, axis=0).astype(jnp.float32),
        precision=lax.Precision.HIGHEST,
        preferred_element_type=jnp.float32,
    )
    base = lax.psum_scatter(base_part, "tensor", scatter_dimension=1, tiled=True)
    mask = jnp.arange(BLK, dtype=jnp.int32)[None, :] < fill[:, None]
    keys = base + delta.reshape(rows, base.shape[1])
    return jnp.where(mask.reshape(rows, 1), keys, 0.0).astype(jnp.bfloat16)


def solution(mesh):
    in_specs = (
        P(("groups", "dp"), "tensor"),
        P("tensor", None),
        P("dp", None, "tensor"),
        P("dp", None, "tensor"),
        P(),
        P("groups", None),
        P("groups"),
    )
    out_specs = P(("groups", "dp"), "tensor")
    planes = dict(mesh.shape) == {"groups": 2, "dp": 8, "tensor": 2}
    return jax.shard_map(
        per_device_planes if planes else per_device_gathered,
        mesh=mesh,
        in_specs=in_specs,
        out_specs=out_specs,
        check_vma=False,
    )
```

```python
import functools

import jax
import jax.numpy as jnp
from jax import lax
from jax.experimental import pallas as pl
from jax.experimental.pallas import tpu as pltpu
from jax.sharding import PartitionSpec as P

ADAPTER_RANK = 64
BLK = 128
FAR_PARTS = 3
SWAP = [(0, 1), (1, 0)]
NT = (((1,), (1,)), ((), ()))
TN = (((0,), (0,)), ((), ()))


def kernel_params(mebibytes):
    return pltpu.CompilerParams(vmem_limit_bytes=mebibytes * 1024 * 1024)


def cost(flops, bytes_accessed):
    return pl.CostEstimate(flops=1, bytes_accessed=1, transcendentals=0)


def after(array, *others):
    return lax.optimization_barrier((array, *others))[0]


SMEM = pl.BlockSpec(memory_space=pltpu.SMEM)
VMEM = pl.BlockSpec(memory_space=pltpu.VMEM)
ANY = pl.BlockSpec(memory_space=pl.ANY)


def base_kernel(cuts, place, tokens, weight, *refs):
    *fars, mine, tokens_v, weight_v, t_sem, w_sem = refs
    rows, half = mine.shape
    part = rows // len(fars)
    copies = []
    for step, (start, depth) in enumerate(cuts):
        span = pl.ds(start, depth)
        token_copy = pltpu.make_async_copy(tokens.at[:, span], tokens_v.at[:, span], t_sem.at[step])
        weight_copy = pltpu.make_async_copy(weight.at[span, :], weight_v.at[span, :], w_sem.at[step])
        token_copy.start()
        weight_copy.start()
        copies.append((token_copy, weight_copy))
    for step, (start, depth) in enumerate(cuts):
        for copy in copies[step]:
            copy.wait()
        outs = [(mine, 0, rows, place[2])]
        outs += [(far, at * part, part, 1 - place[2]) for at, far in enumerate(fars)]
        for out, first, count, core in outs:
            columns = pl.ds(pl.multiple_of(core * half, half), half)
            product = jnp.dot(
                tokens_v[pl.ds(first, count), pl.ds(start, depth)],
                weight_v[pl.ds(start, depth), columns],
                preferred_element_type=jnp.float32,
            )
            out[...] = product if step == 0 else out[...] + product


def base_sums(place, tokens, weight):
    rows, width = tokens.shape
    features = weight.shape[1]
    first = width // 8
    cuts = [(0, first), (first, first)] + [(at * width // 4, width // 4) for at in range(1, 4)]
    far = jax.ShapeDtypeStruct((rows // FAR_PARTS, features // 2), jnp.float32)
    mine = jax.ShapeDtypeStruct((rows, features // 2), jnp.float32)
    return pl.pallas_call(
        functools.partial(base_kernel, cuts),
        in_specs=[SMEM, ANY, ANY],
        out_specs=[VMEM] * (FAR_PARTS + 1),
        out_shape=[far] * FAR_PARTS + [mine],
        scratch_shapes=[
            pltpu.VMEM((rows, width), tokens.dtype),
            pltpu.VMEM((width, features), weight.dtype),
            pltpu.SemaphoreType.DMA((len(cuts),)),
            pltpu.SemaphoreType.DMA((len(cuts),)),
        ],
        compiler_params=kernel_params(52),
        cost_estimate=cost(
            2 * rows * width * features, 2 * width * (rows + features) + 4 * rows * features
        ),
    )(place, tokens, weight)


def pool_of(place, step, other):
    depth = place[1] // 2
    column = place[1] - 2 * depth
    level = lax.rem(depth + 4 - step, 4)
    return 2 * level + (1 - column if other else column)


def half_of(place, kind):
    return {"a": 0, "b": 1, "own": place[0], "far": 1 - place[0]}[kind]


def shrink_kernel(pieces, has_prior, place, pool_index, adapter_index, tokens, *refs):
    refs = list(refs)
    arrays = [refs.pop(0) for _ in range(len({at for _, at, *_ in pieces}))]
    prior = refs.pop(0) if has_prior else None
    sums, tokens_v, sems = refs
    blocks, half = sums.shape[0], tokens_v.shape[3]

    def slot_of(block):
        return pool_index[adapter_index[place[1] * blocks + block]]

    def copy_of(block, side):
        return pltpu.make_async_copy(
            tokens.at[pl.ds(block * BLK, BLK), pl.ds(side * half, half)],
            tokens_v.at[block, side],
            sems.at[block, side],
        )

    def wanted(block, side):
        slot = slot_of(block)
        found = jnp.bool_(False)
        for (step, other, kind), *_ in pieces:
            found |= (slot == pool_of(place, step, other)) & (half_of(place, kind) == side)
        return found

    for block in range(blocks):
        for side in range(2):
            pl.when(wanted(block, side))(copy_of(block, side).start)
    sums[...] = prior[...] if has_prior else jnp.zeros_like(sums)

    def per_block(block, carry):
        slot = slot_of(block)
        for (step, other, kind), at, column, *_ in pieces:

            @pl.when(slot == pool_of(place, step, other))
            def _(kind=kind, at=at, column=column):
                side = half_of(place, kind)
                pltpu.make_async_copy(
                    tokens_v.at[block, side], tokens_v.at[block, side], sems.at[block, side]
                ).wait()
                sums[block] += lax.dot_general(
                    arrays[at][:, column : column + half],
                    tokens_v[block, side],
                    NT,
                    preferred_element_type=jnp.float32,
                )

        return carry

    lax.fori_loop(0, blocks, per_block, 0)


def shrink_sums(scalars, tokens, arrays, pieces, prior=None):
    rows, width = tokens.shape
    blocks = rows // BLK
    has_prior = prior is not None
    return pl.pallas_call(
        functools.partial(shrink_kernel, pieces, has_prior),
        in_specs=[SMEM, SMEM, SMEM, ANY] + [VMEM] * (len(arrays) + has_prior),
        out_specs=VMEM,
        out_shape=jax.ShapeDtypeStruct((blocks, ADAPTER_RANK, BLK), jnp.float32),
        scratch_shapes=[
            pltpu.VMEM((blocks, 2, BLK, width // 2), tokens.dtype),
            pltpu.SemaphoreType.DMA((blocks, 2)),
        ],
        compiler_params=kernel_params(52),
        cost_estimate=cost(rows * width * ADAPTER_RANK * len(pieces), rows * width),
    )(*scalars, tokens, *arrays, *([prior] if has_prior else []))


def select_kernel(pieces, place, pool_index, adapter_index, *refs):
    refs = list(refs)
    arrays = [refs.pop(0) for _ in range(len({at for _, at, _ in pieces}))]
    mine, *fars, base, ups = refs
    part = base.shape[0] // len(fars)
    blocks, _, half = ups.shape
    half = half // 2
    for at, far in enumerate(fars):
        span = slice(at * part, (at + 1) * part)
        base[span, :] = mine[span, :] + far[...]

    def per_block(block, carry):
        slot = pool_index[adapter_index[place[1] * blocks + block]]
        for (step, other, kind), at, column in pieces:

            @pl.when(slot == pool_of(place, step, other))
            def _(kind=kind, at=at, column=column):
                start = pl.multiple_of(half_of(place, kind) * half, half)
                ups[block, :, pl.ds(start, half)] = arrays[at][:, column : column + half]

        return carry

    lax.fori_loop(0, blocks, per_block, 0)


def select_ups(scalars, arrays, pieces, mine, fars):
    rows, half = mine.shape
    blocks = rows // BLK
    return pl.pallas_call(
        functools.partial(select_kernel, pieces),
        in_specs=[SMEM, SMEM, SMEM] + [VMEM] * (len(arrays) + 1 + len(fars)),
        out_specs=[VMEM, VMEM],
        out_shape=[
            jax.ShapeDtypeStruct((rows, half), jnp.float32),
            jax.ShapeDtypeStruct((blocks, ADAPTER_RANK, half), jnp.bfloat16),
        ],
        compiler_params=kernel_params(16),
        cost_estimate=cost(rows * half, 12 * rows * half),
    )(*scalars, *arrays, mine, *fars)


def final_kernel(
    last, place, pool_index, adapter_index, live, base, sums, far_sums, ups, piece, keys, up_v
):
    (step, other, kind), column = last
    blocks, rank, half = ups.shape
    for block in range(blocks):
        index = place[1] * blocks + block
        up_v[...] = ups[block]

        @pl.when(pool_index[adapter_index[index]] == pool_of(place, step, other))
        def _():
            start = pl.multiple_of(half_of(place, kind) * (half // 2), half // 2)
            up_v[:, pl.ds(start, half // 2)] = piece[:, column : column + half // 2]

        total = sums[block] + far_sums[block]
        high = total.astype(jnp.bfloat16)
        rest = total - high.astype(jnp.float32)
        middle = rest.astype(jnp.bfloat16)
        low = (rest - middle.astype(jnp.float32)).astype(jnp.bfloat16)
        up = up_v[...]
        delta = lax.dot_general(
            jnp.concatenate([high, middle, low], axis=0),
            jnp.concatenate([up, up, up], axis=0),
            TN,
            preferred_element_type=jnp.float32,
        )
        row = lax.broadcasted_iota(jnp.int32, (BLK, half), 0)
        span = slice(block * BLK, (block + 1) * BLK)
        keys[span, :] = jnp.where(row < live[index], base[span, :] + delta, 0.0).astype(keys.dtype)


def final_keys(scalars, base, sums, far_sums, ups, piece, last):
    rows, half = base.shape
    return pl.pallas_call(
        functools.partial(final_kernel, last),
        in_specs=[SMEM] * len(scalars) + [VMEM] * 5,
        out_specs=VMEM,
        out_shape=jax.ShapeDtypeStruct((rows, half), jnp.bfloat16),
        scratch_shapes=[pltpu.VMEM((ADAPTER_RANK, half), jnp.bfloat16)],
        compiler_params=kernel_params(12),
        cost_estimate=cost(6 * rows * half * ADAPTER_RANK, 6 * rows * half),
    )(*scalars, base, sums, far_sums, ups, piece)


def per_device_planes(
    tokens,
    key_projection_weight,
    adapter_down_weight,
    adapter_up_weight,
    adapter_pool_index,
    block_adapter_index,
    block_live_tokens,
):
    place = jnp.stack(
        [lax.axis_index("groups"), lax.axis_index("dp"), lax.axis_index("tensor")]
    ).astype(jnp.int32)
    down, up = adapter_down_weight[0], adapter_up_weight[0]
    width, half = down.shape[1] // 2, up.shape[1] // 2
    piece = width + half
    own = jnp.concatenate([down[:, :width], up[:, :half], down[:, width:], up[:, half:]], axis=1)
    first = lax.axis_index("groups") == 0
    own_half = jnp.where(first, own[:, :piece], own[:, piece:])

    def ring(array, step):
        pairs = [(2 * z + y, 2 * ((z + step) % 4) + y) for z in range(4) for y in range(2)]
        return lax.ppermute(array, "dp", pairs)

    def over_y(array):
        return lax.ppermute(array, "dp", [(i, i ^ 1) for i in range(8)])

    def over_x(array):
        return lax.ppermute(array, "groups", SWAP)

    def over_cores(array):
        return lax.ppermute(array, "tensor", SWAP)

    scalars = (place, adapter_pool_index, block_adapter_index[:, 0])
    z1 = ring(own_half, 1)
    y0 = over_y(own)
    z3 = ring(own_half, -1)
    *fars, mine = base_sums(place, tokens, key_projection_weight)
    z1_ = after(z1, mine)
    x1 = over_x(z1_)
    y1 = over_y(z1_)
    z2a = ring(z1_, 1)
    z3_ = after(z3, z1_)
    x3 = over_x(z3_)
    y3 = over_y(after(z3_, y0))
    z2b = ring(x1, 1)
    y2a = over_y(z2a)
    x1y = over_x(y1)
    x3y = over_x(y3)

    sides = [((0, False, "a"), 0, 0), ((0, False, "b"), 0, width),
             ((0, True, "a"), 1, 0), ((0, True, "b"), 1, piece)]
    names = [(1, False, "own"), (1, False, "far"), (3, False, "own"), (3, False, "far"),
             (2, False, "own"), (1, True, "own"), (3, True, "own")]
    sums = shrink_sums(
        scalars,
        after(tokens, z2a),
        [down, y0, z1, x1, z3, x3, z2a, y1, y3],
        sides + [(name, at + 2, 0) for at, name in enumerate(names)],
    )
    y2b = over_y(z2b)
    base_fars = [over_cores(far) for far in fars]
    late_names = [(2, False, "far"), (1, True, "far"), (3, True, "far"), (2, True, "own")]
    late_arrays = [z2b, x1y, x3y, y2a]
    sums = shrink_sums(
        scalars,
        tokens,
        late_arrays,
        [(name, at, 0) for at, name in enumerate(late_names)],
        sums,
    )
    base, ups = select_ups(
        scalars,
        [up, y0, z1, x1, z3, x3, z2a, y1, y3] + late_arrays,
        [((0, False, "a"), 0, 0), ((0, False, "b"), 0, half),
         ((0, True, "a"), 1, width), ((0, True, "b"), 1, piece + width)]
        + [(name, at + 2, width) for at, name in enumerate(names + late_names)],
        mine,
        base_fars,
    )
    last = (2, True, "far")
    sums = shrink_sums(scalars, after(tokens, base), [y2b], [(last, 0, 0)], sums)
    far_sums = over_cores(sums)
    return final_keys(
        (*scalars, block_live_tokens), base, sums, far_sums, ups, y2b, (last, width)
    )


def per_device_gathered(
    tokens,
    key_projection_weight,
    adapter_down_weight,
    adapter_up_weight,
    adapter_pool_index,
    block_adapter_index,
    block_live_tokens,
):
    rows = tokens.shape[0]
    blocks = rows // BLK
    first_block = lax.axis_index("dp") * blocks
    slots = lax.dynamic_slice_in_dim(
        adapter_pool_index[block_adapter_index[:, 0]], first_block, blocks
    )
    fill = lax.dynamic_slice_in_dim(block_live_tokens, first_block, blocks)
    base_part = jnp.dot(tokens, key_projection_weight, preferred_element_type=jnp.float32)
    down = lax.all_gather(adapter_down_weight, "dp", axis=0, tiled=True)
    up = lax.all_gather(adapter_up_weight, "dp", axis=0, tiled=True)
    token_blocks = tokens.reshape(blocks, BLK, tokens.shape[1])
    shrink = jnp.einsum(
        "nrd,nbd->rnb",
        jnp.take(down, slots, axis=0),
        token_blocks,
        preferred_element_type=jnp.float32,
    )
    shrink = lax.psum(shrink.reshape(ADAPTER_RANK, rows), "tensor")
    delta = jnp.einsum(
        "rnb,nrc->nbc",
        shrink.reshape(ADAPTER_RANK, blocks, BLK),
        jnp.take(up, slots, axis=0).astype(jnp.float32),
        precision=lax.Precision.HIGHEST,
        preferred_element_type=jnp.float32,
    )
    base = lax.psum_scatter(base_part, "tensor", scatter_dimension=1, tiled=True)
    mask = jnp.arange(BLK, dtype=jnp.int32)[None, :] < fill[:, None]
    keys = base + delta.reshape(rows, base.shape[1])
    return jnp.where(mask.reshape(rows, 1), keys, 0.0).astype(jnp.bfloat16)


def solution(mesh):
    in_specs = (
        P(("groups", "dp"), "tensor"),
        P("tensor", None),
        P("dp", None, "tensor"),
        P("dp", None, "tensor"),
        P(),
        P("groups", None),
        P("groups"),
    )
    out_specs = P(("groups", "dp"), "tensor")
    planes = dict(mesh.shape) == {"groups": 2, "dp": 8, "tensor": 2}
    return jax.shard_map(
        per_device_planes if planes else per_device_gathered,
        mesh=mesh,
        in_specs=in_specs,
        out_specs=out_specs,
        check_vma=False,
    )
```

```python
import functools

import jax
import jax.numpy as jnp
from jax import lax
from jax.experimental import pallas as pl
from jax.experimental.pallas import tpu as pltpu
from jax.sharding import PartitionSpec as P

ADAPTER_RANK = 64
BLK = 128
FAR_PARTS = 3
SWAP = [(0, 1), (1, 0)]
NT = (((1,), (1,)), ((), ()))
TN = (((0,), (0,)), ((), ()))


def kernel_params(mebibytes):
    return pltpu.CompilerParams(vmem_limit_bytes=mebibytes * 1024 * 1024)


LIGHT = pl.CostEstimate(flops=1, bytes_accessed=1, transcendentals=0)


def after(array, *others):
    return lax.optimization_barrier((array, *others))[0]


SMEM = pl.BlockSpec(memory_space=pltpu.SMEM)
VMEM = pl.BlockSpec(memory_space=pltpu.VMEM)
ANY = pl.BlockSpec(memory_space=pl.ANY)


def base_kernel(cuts, other, place, tokens, weight, *refs):
    *outs, tokens_v, weight_v, t_sem, w_sem = refs
    part, half = outs[0].shape
    core = 1 - place[2] if other else place[2]
    columns = pl.ds(pl.multiple_of(core * half, half), half)
    copies = []
    for step, (start, depth) in enumerate(cuts):
        span = pl.ds(start, depth)
        pair = (
            pltpu.make_async_copy(tokens.at[:, span], tokens_v.at[:, span], t_sem.at[step]),
            pltpu.make_async_copy(weight.at[span, columns], weight_v.at[span, :], w_sem.at[step]),
        )
        for copy in pair:
            copy.start()
        copies.append(pair)
    for step, (start, depth) in enumerate(cuts):
        for copy in copies[step]:
            copy.wait()
        for at, out in enumerate(outs):
            product = jnp.dot(
                tokens_v[pl.ds(at * part, part), pl.ds(start, depth)],
                weight_v[pl.ds(start, depth), :],
                preferred_element_type=jnp.float32,
            )
            out[...] = product if step == 0 else out[...] + product


def base_sums(place, tokens, weight, other, parts):
    rows, width = tokens.shape
    half = weight.shape[1] // 2
    first = width // 8
    cuts = [(0, first), (first, first)] + [(at * width // 4, width // 4) for at in range(1, 4)]
    return pl.pallas_call(
        functools.partial(base_kernel, cuts, other),
        in_specs=[SMEM, ANY, ANY],
        out_specs=[VMEM] * parts,
        out_shape=[jax.ShapeDtypeStruct((rows // parts, half), jnp.float32)] * parts,
        scratch_shapes=[
            pltpu.VMEM((rows, width), tokens.dtype),
            pltpu.VMEM((width, half), weight.dtype),
            pltpu.SemaphoreType.DMA((len(cuts),)),
            pltpu.SemaphoreType.DMA((len(cuts),)),
        ],
        compiler_params=kernel_params(46),
        cost_estimate=LIGHT,
    )(place, tokens, weight)


def pool_of(place, step, other):
    depth = place[1] // 2
    column = place[1] - 2 * depth
    level = lax.rem(depth + 4 - step, 4)
    return 2 * level + (1 - column if other else column)


def half_of(place, kind):
    return {"a": 0, "b": 1, "own": place[0], "far": 1 - place[0]}[kind]


def shrink_kernel(pieces, has_prior, place, pool_index, adapter_index, tokens, *refs):
    refs = list(refs)
    arrays = [refs.pop(0) for _ in range(len({at for _, at, _ in pieces}))]
    prior = refs.pop(0) if has_prior else None
    sums, tokens_v, maps_v, t_sem, m_sem = refs
    blocks, half = sums.shape[0], tokens_v.shape[3]

    def slot_of(block):
        return pool_index[adapter_index[place[1] * blocks + block]]

    def token_copy(block, side):
        return pltpu.make_async_copy(
            tokens.at[pl.ds(block * BLK, BLK), pl.ds(side * half, half)],
            tokens_v.at[block, side],
            t_sem.at[block, side],
        )

    def start(block, carry):
        slot = slot_of(block)
        for (step, other, kind), at, column in pieces:

            @pl.when(slot == pool_of(place, step, other))
            def _(kind=kind, at=at, column=column):
                side = half_of(place, kind)
                token_copy(block, side).start()
                pltpu.make_async_copy(
                    arrays[at].at[:, column : column + half],
                    maps_v.at[block, side],
                    m_sem.at[block, side],
                ).start()

        return carry

    lax.fori_loop(0, blocks, start, 0)
    sums[...] = prior[...] if has_prior else jnp.zeros_like(sums)

    def add(block, carry):
        slot = slot_of(block)
        for side in range(2):
            wanted = jnp.bool_(False)
            for (step, other, kind), *_ in pieces:
                same = half_of(place, kind) == side
                wanted |= (slot == pool_of(place, step, other)) & same

            @pl.when(wanted)
            def _(side=side):
                token_copy(block, side).wait()
                pltpu.make_async_copy(
                    maps_v.at[block, side], maps_v.at[block, side], m_sem.at[block, side]
                ).wait()
                sums[block] += lax.dot_general(
                    maps_v[block, side],
                    tokens_v[block, side],
                    NT,
                    preferred_element_type=jnp.float32,
                )

        return carry

    lax.fori_loop(0, blocks, add, 0)


def shrink_sums(scalars, tokens, arrays, pieces, prior=None):
    rows, width = tokens.shape
    blocks, half = rows // BLK, width // 2
    has_prior = prior is not None
    return pl.pallas_call(
        functools.partial(shrink_kernel, pieces, has_prior),
        in_specs=[SMEM, SMEM, SMEM, ANY] + [ANY] * len(arrays) + [VMEM] * has_prior,
        out_specs=VMEM,
        out_shape=jax.ShapeDtypeStruct((blocks, ADAPTER_RANK, BLK), jnp.float32),
        scratch_shapes=[
            pltpu.VMEM((blocks, 2, BLK, half), tokens.dtype),
            pltpu.VMEM((blocks, 2, ADAPTER_RANK, half), tokens.dtype),
            pltpu.SemaphoreType.DMA((blocks, 2)),
            pltpu.SemaphoreType.DMA((blocks, 2)),
        ],
        compiler_params=kernel_params(46),
        cost_estimate=LIGHT,
    )(*scalars, tokens, *arrays, *([prior] if has_prior else []))


def select_kernel(pieces, place, pool_index, adapter_index, *refs):
    *arrays, ups, sem = refs
    blocks, _, half = ups.shape
    half = half // 2

    def copies(block, act):
        slot = pool_index[adapter_index[place[1] * blocks + block]]
        for (step, other, kind), at, column in pieces:

            @pl.when(slot == pool_of(place, step, other))
            def _(kind=kind, at=at, column=column):
                side = half_of(place, kind)
                start = pl.multiple_of(side * half, half)
                act(
                    pltpu.make_async_copy(
                        arrays[at].at[:, column : column + half],
                        ups.at[block, :, pl.ds(start, half)],
                        sem.at[block, side],
                    )
                )

    def start(block, carry):
        copies(block, lambda copy: copy.start())
        return carry

    def wait(block, carry):
        copies(block, lambda copy: copy.wait())
        return carry

    lax.fori_loop(0, blocks, start, 0)
    lax.fori_loop(0, blocks, wait, 0)


def select_ups(scalars, arrays, pieces, blocks, half):
    return pl.pallas_call(
        functools.partial(select_kernel, pieces),
        in_specs=[SMEM, SMEM, SMEM] + [ANY] * len(arrays),
        out_specs=VMEM,
        out_shape=jax.ShapeDtypeStruct((blocks, ADAPTER_RANK, half), jnp.bfloat16),
        scratch_shapes=[pltpu.SemaphoreType.DMA((blocks, 2))],
        compiler_params=kernel_params(16),
        cost_estimate=LIGHT,
    )(*scalars, *arrays)


def final_kernel(
    last, place, pool_index, adapter_index, live, base, sums, far_sums, ups, piece, keys, up_v
):
    (step, other, kind), column = last
    blocks, rank, half = ups.shape
    for block in range(blocks):
        index = place[1] * blocks + block
        up_v[...] = ups[block]

        @pl.when(pool_index[adapter_index[index]] == pool_of(place, step, other))
        def _():
            start = pl.multiple_of(half_of(place, kind) * (half // 2), half // 2)
            up_v[:, pl.ds(start, half // 2)] = piece[:, column : column + half // 2]

        total = sums[block] + far_sums[block]
        high = total.astype(jnp.bfloat16)
        rest = total - high.astype(jnp.float32)
        middle = rest.astype(jnp.bfloat16)
        low = (rest - middle.astype(jnp.float32)).astype(jnp.bfloat16)
        up = up_v[...]
        delta = lax.dot_general(
            jnp.concatenate([high, middle, low], axis=0),
            jnp.concatenate([up, up, up], axis=0),
            TN,
            preferred_element_type=jnp.float32,
        )
        row = lax.broadcasted_iota(jnp.int32, (BLK, half), 0)
        span = slice(block * BLK, (block + 1) * BLK)
        keys[span, :] = jnp.where(row < live[index], base[span, :] + delta, 0.0).astype(keys.dtype)


def final_keys(scalars, base, sums, far_sums, ups, piece, last):
    rows, half = base.shape
    return pl.pallas_call(
        functools.partial(final_kernel, last),
        in_specs=[SMEM] * len(scalars) + [VMEM] * 5,
        out_specs=VMEM,
        out_shape=jax.ShapeDtypeStruct((rows, half), jnp.bfloat16),
        scratch_shapes=[pltpu.VMEM((ADAPTER_RANK, half), jnp.bfloat16)],
        compiler_params=kernel_params(12),
        cost_estimate=LIGHT,
    )(*scalars, base, sums, far_sums, ups, piece)


def per_device_planes(
    tokens,
    key_projection_weight,
    adapter_down_weight,
    adapter_up_weight,
    adapter_pool_index,
    block_adapter_index,
    block_live_tokens,
):
    place = jnp.stack(
        [lax.axis_index("groups"), lax.axis_index("dp"), lax.axis_index("tensor")]
    ).astype(jnp.int32)
    down, up = adapter_down_weight[0], adapter_up_weight[0]
    width, half = down.shape[1] // 2, up.shape[1] // 2
    piece = width + half
    own = jnp.concatenate([down[:, :width], up[:, :half], down[:, width:], up[:, half:]], axis=1)
    first = lax.axis_index("groups") == 0
    own_half = jnp.where(first, own[:, :piece], own[:, piece:])

    def ring(array, step):
        pairs = [(2 * z + y, 2 * ((z + step) % 4) + y) for z in range(4) for y in range(2)]
        return lax.ppermute(array, "dp", pairs)

    def over_y(array):
        return lax.ppermute(array, "dp", [(i, i ^ 1) for i in range(8)])

    def over_x(array):
        return lax.ppermute(array, "groups", SWAP)

    def over_cores(array):
        return lax.ppermute(array, "tensor", SWAP)

    scalars = (place, adapter_pool_index, block_adapter_index[:, 0])
    z1 = ring(own_half, 1)
    y0 = over_y(own)
    z3 = ring(own_half, -1)
    fars = base_sums(place, tokens, key_projection_weight, True, FAR_PARTS)
    z1_ = after(z1, fars[0])
    x1 = over_x(z1_)
    y1 = over_y(z1_)
    z2a = ring(z1_, 1)
    z3_ = after(z3, z1_)
    x3 = over_x(z3_)
    y3 = over_y(after(z3_, y0))
    (mine,) = base_sums(place, after(tokens, z3_, y0), key_projection_weight, False, 1)
    z2b = ring(after(x1, mine), 1)
    y2a = over_y(after(z2a, mine))
    x1y = over_x(y1)
    x3y = over_x(y3)
    base_fars = [over_cores(far) for far in fars]

    group_1 = [
        ((0, False, "a"), 0, 0),
        ((0, False, "b"), 0, width),
        ((0, True, "a"), 1, 0),
        ((0, True, "b"), 1, piece),
        ((1, False, "own"), 2, 0),
        ((3, False, "own"), 3, 0),
    ]
    group_2 = [
        ((1, False, "far"), 0, 0),
        ((1, True, "own"), 1, 0),
        ((2, False, "own"), 2, 0),
        ((3, False, "far"), 3, 0),
        ((3, True, "own"), 4, 0),
    ]
    group_3 = [
        ((2, False, "far"), 0, 0),
        ((1, True, "far"), 1, 0),
        ((3, True, "far"), 2, 0),
        ((2, True, "own"), 3, 0),
    ]
    last = (2, True, "far")
    arrays_1, arrays_2, arrays_3 = [down, y0, z1, z3], [x1, y1, z2a, x3, y3], [z2b, x1y, x3y, y2a]
    sums = shrink_sums(scalars, after(tokens, y1, z2a, mine), arrays_1, group_1)
    y2b = over_y(after(z2b, x1y, x3y, y2a))
    sums = shrink_sums(scalars, after(tokens, z2b), arrays_2, group_2, sums)
    sums = shrink_sums(scalars, tokens, arrays_3, group_3, sums)
    up_group = [((0, False, "a"), 0, 0), ((0, False, "b"), 0, half)]
    up_group += [((0, True, "a"), 1, width), ((0, True, "b"), 1, piece + width)]
    up_group += [(name, at, width) for name, at, _ in group_1[4:]]
    up_group += [(name, at + 4, width) for name, at, _ in group_2]
    up_group += [(name, at + 9, width) for name, at, _ in group_3]
    ups = select_ups(
        scalars,
        [up] + arrays_1[1:] + arrays_2 + arrays_3,
        up_group,
        tokens.shape[0] // BLK,
        up.shape[1],
    )
    base = mine + jnp.concatenate(base_fars, axis=0)
    sums = shrink_sums(scalars, after(tokens, base, ups), [y2b], [(last, 0, 0)], sums)
    far_sums = over_cores(sums)
    return final_keys(
        (*scalars, block_live_tokens), base, sums, far_sums, ups, y2b, (last, width)
    )


def per_device_gathered(
    tokens,
    key_projection_weight,
    adapter_down_weight,
    adapter_up_weight,
    adapter_pool_index,
    block_adapter_index,
    block_live_tokens,
):
    rows = tokens.shape[0]
    blocks = rows // BLK
    first_block = lax.axis_index("dp") * blocks
    slots = lax.dynamic_slice_in_dim(
        adapter_pool_index[block_adapter_index[:, 0]], first_block, blocks
    )
    fill = lax.dynamic_slice_in_dim(block_live_tokens, first_block, blocks)
    base_part = jnp.dot(tokens, key_projection_weight, preferred_element_type=jnp.float32)
    down = lax.all_gather(adapter_down_weight, "dp", axis=0, tiled=True)
    up = lax.all_gather(adapter_up_weight, "dp", axis=0, tiled=True)
    token_blocks = tokens.reshape(blocks, BLK, tokens.shape[1])
    shrink = jnp.einsum(
        "nrd,nbd->rnb",
        jnp.take(down, slots, axis=0),
        token_blocks,
        preferred_element_type=jnp.float32,
    )
    shrink = lax.psum(shrink.reshape(ADAPTER_RANK, rows), "tensor")
    delta = jnp.einsum(
        "rnb,nrc->nbc",
        shrink.reshape(ADAPTER_RANK, blocks, BLK),
        jnp.take(up, slots, axis=0).astype(jnp.float32),
        precision=lax.Precision.HIGHEST,
        preferred_element_type=jnp.float32,
    )
    base = lax.psum_scatter(base_part, "tensor", scatter_dimension=1, tiled=True)
    mask = jnp.arange(BLK, dtype=jnp.int32)[None, :] < fill[:, None]
    keys = base + delta.reshape(rows, base.shape[1])
    return jnp.where(mask.reshape(rows, 1), keys, 0.0).astype(jnp.bfloat16)


def solution(mesh):
    in_specs = (
        P(("groups", "dp"), "tensor"),
        P("tensor", None),
        P("dp", None, "tensor"),
        P("dp", None, "tensor"),
        P(),
        P("groups", None),
        P("groups"),
    )
    out_specs = P(("groups", "dp"), "tensor")
    planes = dict(mesh.shape) == {"groups": 2, "dp": 8, "tensor": 2}
    return jax.shard_map(
        per_device_planes if planes else per_device_gathered,
        mesh=mesh,
        in_specs=in_specs,
        out_specs=out_specs,
        check_vma=False,
    )
```

```python
import functools

import jax
import jax.numpy as jnp
from jax import lax
from jax.experimental import pallas as pl
from jax.experimental.pallas import tpu as pltpu
from jax.sharding import PartitionSpec as P

ADAPTER_RANK = 64
BLK = 128
FAR_PARTS = 3
SWAP = [(0, 1), (1, 0)]
NT = (((1,), (1,)), ((), ()))
TN = (((0,), (0,)), ((), ()))


def kernel_params(mebibytes):
    return pltpu.CompilerParams(vmem_limit_bytes=mebibytes * 1024 * 1024)


LIGHT = pl.CostEstimate(flops=1, bytes_accessed=1, transcendentals=0)


HEAVY = pl.CostEstimate(flops=30000000000, bytes_accessed=1, transcendentals=0)


def after(array, *others):
    return lax.optimization_barrier((array, *others))[0]


SMEM = pl.BlockSpec(memory_space=pltpu.SMEM)
VMEM = pl.BlockSpec(memory_space=pltpu.VMEM)
ANY = pl.BlockSpec(memory_space=pl.ANY)


def base_kernel(cuts, other, place, tokens, weight, *refs):
    *outs, tokens_v, weight_v, t_sem, w_sem = refs
    base_steps(cuts, 1 - place[2] if other else place[2], tokens, weight, outs, refs[-4:])


def base_steps(cuts, core, tokens, weight, outs, scratch):
    tokens_v, weight_v, t_sem, w_sem = scratch
    part, half = outs[0].shape
    columns = pl.ds(pl.multiple_of(core * half, half), half)
    copies = []
    for step, (start, depth) in enumerate(cuts):
        span = pl.ds(start, depth)
        pair = (
            pltpu.make_async_copy(tokens.at[:, span], tokens_v.at[:, span], t_sem.at[step]),
            pltpu.make_async_copy(weight.at[span, columns], weight_v.at[span, :], w_sem.at[step]),
        )
        for copy in pair:
            copy.start()
        copies.append(pair)
    for step, (start, depth) in enumerate(cuts):
        for copy in copies[step]:
            copy.wait()
        for at, out in enumerate(outs):
            product = jnp.dot(
                tokens_v[pl.ds(at * part, part), pl.ds(start, depth)],
                weight_v[pl.ds(start, depth), :],
                preferred_element_type=jnp.float32,
            )
            out[...] = product if step == 0 else out[...] + product


def base_cuts(width):
    first = width // 8
    return [(0, first), (first, first)] + [(at * width // 4, width // 4) for at in range(1, 4)]


def base_scratch(tokens, weight):
    rows, width = tokens.shape
    steps = len(base_cuts(width))
    return [
        pltpu.VMEM((rows, width), tokens.dtype),
        pltpu.VMEM((width, weight.shape[1] // 2), weight.dtype),
        pltpu.SemaphoreType.DMA((steps,)),
        pltpu.SemaphoreType.DMA((steps,)),
    ]


def base_far(place, tokens, weight, parts):
    rows, width = tokens.shape
    half = weight.shape[1] // 2
    return pl.pallas_call(
        functools.partial(base_kernel, base_cuts(width), True),
        in_specs=[SMEM, ANY, ANY],
        out_specs=[VMEM] * parts,
        out_shape=[jax.ShapeDtypeStruct((rows // parts, half), jnp.float32)] * parts,
        scratch_shapes=base_scratch(tokens, weight),
        compiler_params=kernel_params(50),
        cost_estimate=HEAVY,
    )(place, tokens, weight)


def entry_of(place, slot):
    back = ((place[1] >> 1) - (slot >> 1)) & 3
    return 2 * back + ((slot ^ place[1]) & 1)


def side_of(place, kind):
    return {"a": 0, "b": 1, "own": place[0], "far": 1 - place[0]}[kind]


def start_maps(pieces, entry_at, place, downs, ups, maps_v, up_map, sems, start_tokens=None):
    m_sem, u_sem = sems
    blocks, _, _, wide = maps_v.shape
    half = up_map.shape[2] // 2

    def start(block, carry):
        entry = entry_at(block)
        for at_entry, kind, at, column, up_column in pieces:

            @pl.when(entry == at_entry)
            def _(kind=kind, at=at, column=column, up_column=up_column):
                side = side_of(place, kind)
                if start_tokens is not None:
                    start_tokens(block, side)
                pltpu.make_async_copy(
                    downs[at].at[:, column : column + wide],
                    maps_v.at[block, side],
                    m_sem.at[block, side],
                ).start()
                pltpu.make_async_copy(
                    ups[at].at[:, up_column : up_column + half],
                    up_map.at[block, :, pl.ds(pl.multiple_of(side * half, half), half)],
                    u_sem.at[block, side],
                ).start()

        return carry

    lax.fori_loop(0, blocks, start, 0)


def add_maps(pieces, entry_at, place, maps_v, tokens_v, up_map, sums, sems, wait_tokens=None):
    m_sem, u_sem = sems
    blocks, _, _, wide = maps_v.shape
    half = up_map.shape[2] // 2
    masks = []
    for side in range(2):
        bits = {"a": 0, "b": 0, "own": 0, "far": 0}
        for entry, kind, *_ in pieces:
            bits[kind] |= 1 << entry
        masks.append(
            bits["a" if side == 0 else "b"]
            | jnp.where(place[0] == side, bits["own"], bits["far"])
        )

    def add(block, carry):
        entry = entry_at(block)
        for side in range(2):

            @pl.when(((masks[side] >> entry) & 1) == 1)
            def _(side=side):
                if wait_tokens is not None:
                    wait_tokens(block, side)
                pltpu.make_async_copy(
                    maps_v.at[block, side], maps_v.at[block, side], m_sem.at[block, side]
                ).wait()
                sums[block] += lax.dot_general(
                    maps_v[block, side],
                    tokens_v[pl.ds(pl.multiple_of(block * BLK, BLK), BLK), pl.ds(side * wide, wide)],
                    NT,
                    preferred_element_type=jnp.float32,
                )
                half_map = up_map.at[block, :, pl.ds(side * half, half)]
                pltpu.make_async_copy(half_map, half_map, u_sem.at[block, side]).wait()

        return carry

    lax.fori_loop(0, blocks, add, 0)


def mine_kernel(cuts, pieces, count, place, pool_index, adapter_index, tokens, weight, *refs):
    downs, ups = refs[:count], refs[count : 2 * count]
    mine, sums, up_map, tokens_v, weight_v, t_sem, w_sem, maps_v, m_sem, u_sem = refs[2 * count :]
    blocks = sums.shape[0]

    def entry_at(block):
        return entry_of(place, pool_index[adapter_index[place[1] * blocks + block]])

    start_maps(pieces, entry_at, place, downs, ups, maps_v, up_map, (m_sem, u_sem))
    base_steps(cuts, place[2], tokens, weight, [mine], (tokens_v, weight_v, t_sem, w_sem))
    sums[...] = jnp.zeros_like(sums)
    add_maps(pieces, entry_at, place, maps_v, tokens_v, up_map, sums, (m_sem, u_sem))


def map_scratch(blocks, wide, dtype):
    return [
        pltpu.VMEM((blocks, 2, ADAPTER_RANK, wide), dtype),
        pltpu.SemaphoreType.DMA((blocks, 2)),
        pltpu.SemaphoreType.DMA((blocks, 2)),
    ]


def base_mine(scalars, tokens, weight, downs, ups, pieces):
    rows, width = tokens.shape
    blocks, half = rows // BLK, weight.shape[1] // 2
    return pl.pallas_call(
        functools.partial(mine_kernel, base_cuts(width), pieces, len(downs)),
        in_specs=[SMEM, SMEM, SMEM] + [ANY] * (2 + 2 * len(downs)),
        out_specs=[VMEM, VMEM, ANY],
        out_shape=[
            jax.ShapeDtypeStruct((rows, half), jnp.float32),
            jax.ShapeDtypeStruct((blocks, ADAPTER_RANK, BLK), jnp.float32),
            jax.ShapeDtypeStruct((blocks, ADAPTER_RANK, half), jnp.bfloat16),
        ],
        scratch_shapes=base_scratch(tokens, weight) + map_scratch(blocks, width // 2, tokens.dtype),
        compiler_params=kernel_params(50),
        cost_estimate=HEAVY,
    )(*scalars, tokens, weight, *downs, *ups)


def shrink_kernel(pieces, count, place, pool_index, adapter_index, tokens, *refs):
    arrays = refs[:count]
    prior, _, sums, up_map, tokens_v, t_sem, maps_v, m_sem, u_sem = refs[count:]
    blocks, wide = sums.shape[0], maps_v.shape[3]

    def entry_at(block):
        return entry_of(place, pool_index[adapter_index[place[1] * blocks + block]])

    def token_copy(block, side):
        place_of = (
            pl.ds(pl.multiple_of(block * BLK, BLK), BLK),
            pl.ds(pl.multiple_of(side * wide, wide), wide),
        )
        return pltpu.make_async_copy(
            tokens.at[place_of], tokens_v.at[place_of], t_sem.at[block, side]
        )

    start_maps(
        pieces, entry_at, place, arrays, arrays, maps_v, up_map, (m_sem, u_sem),
        lambda block, side: token_copy(block, side).start(),
    )
    sums[...] = prior[...]
    add_maps(
        pieces, entry_at, place, maps_v, tokens_v, up_map, sums, (m_sem, u_sem),
        lambda block, side: token_copy(block, side).wait(),
    )


def shrink_sums(scalars, tokens, arrays, pieces, sums, up_map):
    rows, width = tokens.shape
    blocks = rows // BLK
    count = len(arrays)
    return pl.pallas_call(
        functools.partial(shrink_kernel, pieces, count),
        in_specs=[SMEM, SMEM, SMEM] + [ANY] * (1 + count) + [VMEM, ANY],
        out_specs=[VMEM, ANY],
        out_shape=[
            jax.ShapeDtypeStruct(sums.shape, sums.dtype),
            jax.ShapeDtypeStruct(up_map.shape, up_map.dtype),
        ],
        input_output_aliases={5 + count: 1},
        scratch_shapes=[
            pltpu.VMEM((rows, width), tokens.dtype),
            pltpu.SemaphoreType.DMA((blocks, 2)),
        ]
        + map_scratch(blocks, width // 2, tokens.dtype),
        compiler_params=kernel_params(50),
        cost_estimate=HEAVY,
    )(*scalars, tokens, *arrays, sums, up_map)


def final_kernel(place, live, base, sums, far_sums, ups, keys):
    blocks, _, half = ups.shape
    for block in range(blocks):
        total = sums[block] + far_sums[block]
        high = total.astype(jnp.bfloat16)
        rest = total - high.astype(jnp.float32)
        middle = rest.astype(jnp.bfloat16)
        low = (rest - middle.astype(jnp.float32)).astype(jnp.bfloat16)
        up = ups[block]
        delta = lax.dot_general(
            jnp.concatenate([high, middle, low], axis=0),
            jnp.concatenate([up, up, up], axis=0),
            TN,
            preferred_element_type=jnp.float32,
        )
        row = lax.broadcasted_iota(jnp.int32, (BLK, half), 0)
        fill = live[place[1] * blocks + block]
        span = slice(block * BLK, (block + 1) * BLK)
        keys[span, :] = jnp.where(row < fill, base[span, :] + delta, 0.0).astype(keys.dtype)


def final_keys(place, live, base, sums, far_sums, ups):
    rows, half = base.shape
    return pl.pallas_call(
        final_kernel,
        in_specs=[SMEM, SMEM] + [VMEM] * 4,
        out_specs=VMEM,
        out_shape=jax.ShapeDtypeStruct((rows, half), jnp.bfloat16),
        compiler_params=kernel_params(12),
        cost_estimate=LIGHT,
    )(place, live, base, sums, far_sums, ups)


def per_device_planes(
    tokens,
    key_projection_weight,
    adapter_down_weight,
    adapter_up_weight,
    adapter_pool_index,
    block_adapter_index,
    block_live_tokens,
):
    place = jnp.stack(
        [lax.axis_index("groups"), lax.axis_index("dp"), lax.axis_index("tensor")]
    ).astype(jnp.int32)
    down, up = adapter_down_weight[0], adapter_up_weight[0]
    width, half = down.shape[1] // 2, up.shape[1] // 2
    piece = width + half
    own = jnp.concatenate([down[:, :width], up[:, :half], down[:, width:], up[:, half:]], axis=1)
    first = lax.axis_index("groups") == 0
    own_half = jnp.where(first, own[:, :piece], own[:, piece:])

    def ring(array, step):
        pairs = [(2 * z + y, 2 * ((z + step) % 4) + y) for z in range(4) for y in range(2)]
        return lax.ppermute(array, "dp", pairs)

    def over_y(array):
        return lax.ppermute(array, "dp", [(i, i ^ 1) for i in range(8)])

    def over_x(array):
        return lax.ppermute(array, "groups", SWAP)

    def over_cores(array):
        return lax.ppermute(array, "tensor", SWAP)

    scalars = (place, adapter_pool_index, block_adapter_index[:, 0])
    weight = key_projection_weight
    z1 = ring(own_half, 1)
    y0 = over_y(own)
    z3 = ring(own_half, -1)
    fars = base_far(place, tokens, weight, FAR_PARTS)
    z1_ = after(z1, fars[0])
    x1 = over_x(z1_)
    y1 = over_y(z1_)
    z2a = ring(z1_, 1)
    z3_ = after(z3, z1_)
    x3 = over_x(z3_)
    y3 = over_y(after(z3_, y0))
    mine, sums, ups = base_mine(
        scalars,
        after(tokens, z3_, y0),
        weight,
        [down, y0, z1, z3],
        [up, y0, z1, z3],
        [
            (0, "a", 0, 0, 0),
            (0, "b", 0, width, half),
            (1, "a", 1, 0, width),
            (1, "b", 1, piece, piece + width),
            (2, "own", 2, 0, width),
            (6, "own", 3, 0, width),
        ],
    )

    def add_terms(tokens, named, sums, ups):
        pieces = [(entry, kind, at, 0, width) for at, (entry, kind, _) in enumerate(named)]
        return shrink_sums(scalars, tokens, [array for *_, array in named], pieces, sums, ups)

    z2b = ring(after(x1, mine), 1)
    y2a = over_y(z2a)
    x1y = over_x(y1)
    x3y = over_x(y3)
    sums, ups = add_terms(
        after(tokens, mine),
        [(2, "far", x1), (3, "own", y1), (4, "own", z2a), (6, "far", x3), (7, "own", y3)],
        sums,
        ups,
    )
    base_fars = [over_cores(after(far, sums)) for far in fars]
    y2b = over_y(after(z2b, sums))
    base = mine + jnp.concatenate(base_fars, axis=0)
    sums, ups = add_terms(
        tokens, [(4, "far", z2b), (3, "far", x1y), (7, "far", x3y), (5, "own", y2a)], sums, ups
    )
    sums, ups = add_terms(after(tokens, base), [(5, "far", y2b)], sums, ups)
    far_sums = over_cores(sums)
    return final_keys(place, block_live_tokens, base, sums, far_sums, ups)


def per_device_gathered(
    tokens,
    key_projection_weight,
    adapter_down_weight,
    adapter_up_weight,
    adapter_pool_index,
    block_adapter_index,
    block_live_tokens,
):
    rows = tokens.shape[0]
    blocks = rows // BLK
    first_block = lax.axis_index("dp") * blocks
    slots = lax.dynamic_slice_in_dim(
        adapter_pool_index[block_adapter_index[:, 0]], first_block, blocks
    )
    fill = lax.dynamic_slice_in_dim(block_live_tokens, first_block, blocks)
    base_part = jnp.dot(tokens, key_projection_weight, preferred_element_type=jnp.float32)
    down = lax.all_gather(adapter_down_weight, "dp", axis=0, tiled=True)
    up = lax.all_gather(adapter_up_weight, "dp", axis=0, tiled=True)
    token_blocks = tokens.reshape(blocks, BLK, tokens.shape[1])
    shrink = jnp.einsum(
        "nrd,nbd->rnb",
        jnp.take(down, slots, axis=0),
        token_blocks,
        preferred_element_type=jnp.float32,
    )
    shrink = lax.psum(shrink.reshape(ADAPTER_RANK, rows), "tensor")
    delta = jnp.einsum(
        "rnb,nrc->nbc",
        shrink.reshape(ADAPTER_RANK, blocks, BLK),
        jnp.take(up, slots, axis=0).astype(jnp.float32),
        precision=lax.Precision.HIGHEST,
        preferred_element_type=jnp.float32,
    )
    base = lax.psum_scatter(base_part, "tensor", scatter_dimension=1, tiled=True)
    mask = jnp.arange(BLK, dtype=jnp.int32)[None, :] < fill[:, None]
    keys = base + delta.reshape(rows, base.shape[1])
    return jnp.where(mask.reshape(rows, 1), keys, 0.0).astype(jnp.bfloat16)


def solution(mesh):
    in_specs = (
        P(("groups", "dp"), "tensor"),
        P("tensor", None),
        P("dp", None, "tensor"),
        P("dp", None, "tensor"),
        P(),
        P("groups", None),
        P("groups"),
    )
    out_specs = P(("groups", "dp"), "tensor")
    planes = dict(mesh.shape) == {"groups": 2, "dp": 8, "tensor": 2}
    return jax.shard_map(
        per_device_planes if planes else per_device_gathered,
        mesh=mesh,
        in_specs=in_specs,
        out_specs=out_specs,
        check_vma=False,
    )
```

```python
import functools

import jax
import jax.numpy as jnp
from jax import lax
from jax.experimental import pallas as pl
from jax.experimental.pallas import tpu as pltpu
from jax.sharding import PartitionSpec as P

ADAPTER_RANK = 64
BLK = 128
FAR_PARTS = 3
SWAP = [(0, 1), (1, 0)]
NT = (((1,), (1,)), ((), ()))
TN = (((0,), (0,)), ((), ()))


def kernel_params(mebibytes):
    return pltpu.CompilerParams(vmem_limit_bytes=mebibytes * 1024 * 1024)


LIGHT = pl.CostEstimate(flops=1, bytes_accessed=1, transcendentals=0)
HEAVY = pl.CostEstimate(flops=30000000000, bytes_accessed=1, transcendentals=0)


def after(array, *others):
    return lax.optimization_barrier((array, *others))[0]


SMEM = pl.BlockSpec(memory_space=pltpu.SMEM)
VMEM = pl.BlockSpec(memory_space=pltpu.VMEM)
ANY = pl.BlockSpec(memory_space=pl.ANY)


def base_kernel(cuts, other, place, tokens, weight, *refs):
    core = 1 - place[2] if other else place[2]
    base_steps(cuts, core, tokens, weight, refs[:-4], refs[-4:])


def base_steps(cuts, core, tokens, weight, outs, scratch):
    tokens_v, weight_v, t_sem, w_sem = scratch
    part, half = outs[0].shape
    columns = pl.ds(pl.multiple_of(core * half, half), half)
    copies = []
    for step, (start, depth) in enumerate(cuts):
        span = pl.ds(start, depth)
        pair = (
            pltpu.make_async_copy(tokens.at[:, span], tokens_v.at[:, span], t_sem.at[step]),
            pltpu.make_async_copy(weight.at[span, columns], weight_v.at[span, :], w_sem.at[step]),
        )
        for copy in pair:
            copy.start()
        copies.append(pair)
    for step, (start, depth) in enumerate(cuts):
        for copy in copies[step]:
            copy.wait()
        for at, out in enumerate(outs):
            product = jnp.dot(
                tokens_v[pl.ds(at * part, part), pl.ds(start, depth)],
                weight_v[pl.ds(start, depth), :],
                preferred_element_type=jnp.float32,
            )
            out[...] = product if step == 0 else out[...] + product


def base_cuts(width):
    eighth = width // 8
    return [(0, eighth)] + [(at * eighth, 2 * eighth) for at in (1, 3, 5)] + [(7 * eighth, eighth)]


def base_scratch(tokens, weight):
    rows, width = tokens.shape
    steps = len(base_cuts(width))
    return [
        pltpu.VMEM((rows, width), tokens.dtype),
        pltpu.VMEM((width, weight.shape[1] // 2), weight.dtype),
        pltpu.SemaphoreType.DMA((steps,)),
        pltpu.SemaphoreType.DMA((steps,)),
    ]


def base_sums(place, tokens, weight, other, parts, hint):
    rows, width = tokens.shape
    half = weight.shape[1] // 2
    return pl.pallas_call(
        functools.partial(base_kernel, base_cuts(width), other),
        in_specs=[SMEM, ANY, ANY],
        out_specs=[VMEM] * parts,
        out_shape=[jax.ShapeDtypeStruct((rows // parts, half), jnp.float32)] * parts,
        scratch_shapes=base_scratch(tokens, weight),
        compiler_params=kernel_params(50),
        cost_estimate=hint,
    )(place, tokens, weight)


def entry_of(place, slot):
    back = ((place[1] >> 1) - (slot >> 1)) & 3
    return 2 * back + ((slot ^ place[1]) & 1)


def side_of(place, kind):
    return {"a": 0, "b": 1, "own": place[0], "far": 1 - place[0]}[kind]


def start_maps(pieces, entry_at, place, arrays, maps_v, up_map, sems, start_tokens):
    m_sem, u_sem = sems
    blocks, _, _, wide = maps_v.shape

    def start(block, carry):
        entry = entry_at(block)
        for at_entry, kind, (at, column), (up_at, up_column), half in pieces:

            @pl.when(entry == at_entry)
            def _(kind=kind, at=at, column=column, up_at=up_at, up_column=up_column):
                side = side_of(place, kind)
                start_tokens(block, side)
                pltpu.make_async_copy(
                    arrays[at].at[:, column : column + wide],
                    maps_v.at[block, side],
                    m_sem.at[block, side],
                ).start()
                pltpu.make_async_copy(
                    arrays[up_at].at[:, up_column : up_column + half],
                    up_map.at[block, :, pl.ds(pl.multiple_of(side * half, half), half)],
                    u_sem.at[block, side],
                ).start()

        return carry

    lax.fori_loop(0, blocks, start, 0)


def add_maps(pieces, entry_at, place, maps_v, tokens_v, up_map, sums, sems, wait_tokens):
    m_sem, u_sem = sems
    blocks, _, _, wide = maps_v.shape
    half = up_map.shape[2] // 2
    masks = []
    for side in range(2):
        bits = {"a": 0, "b": 0, "own": 0, "far": 0}
        for entry, kind, *_ in pieces:
            bits[kind] |= 1 << entry
        masks.append(
            bits["a" if side == 0 else "b"]
            | jnp.where(place[0] == side, bits["own"], bits["far"])
        )

    def add(block, carry):
        entry = entry_at(block)
        for side in range(2):

            @pl.when(((masks[side] >> entry) & 1) == 1)
            def _(side=side):
                wait_tokens(block, side)
                pltpu.make_async_copy(
                    maps_v.at[block, side], maps_v.at[block, side], m_sem.at[block, side]
                ).wait()
                sums[block] += lax.dot_general(
                    maps_v[block, side],
                    tokens_v[pl.ds(pl.multiple_of(block * BLK, BLK), BLK), pl.ds(side * wide, wide)],
                    NT,
                    preferred_element_type=jnp.float32,
                )
                half_map = up_map.at[block, :, pl.ds(side * half, half)]
                pltpu.make_async_copy(half_map, half_map, u_sem.at[block, side]).wait()

        return carry

    lax.fori_loop(0, blocks, add, 0)


def map_scratch(blocks, wide, dtype):
    return [
        pltpu.VMEM((blocks, 2, ADAPTER_RANK, wide), dtype),
        pltpu.SemaphoreType.DMA((blocks, 2)),
        pltpu.SemaphoreType.DMA((blocks, 2)),
    ]


def shrink_kernel(pieces, count, prior_count, place, pool_index, adapter_index, tokens, *refs):
    arrays, priors = refs[:count], refs[count : count + prior_count]
    sums, up_map, tokens_v, t_sem, maps_v, m_sem, u_sem = refs[count + prior_count :]
    blocks, wide = sums.shape[0], maps_v.shape[3]

    def entry_at(block):
        return entry_of(place, pool_index[adapter_index[place[1] * blocks + block]])

    def token_copy(block, side):
        place_of = (
            pl.ds(pl.multiple_of(block * BLK, BLK), BLK),
            pl.ds(pl.multiple_of(side * wide, wide), wide),
        )
        return pltpu.make_async_copy(
            tokens.at[place_of], tokens_v.at[place_of], t_sem.at[block, side]
        )

    start_maps(
        pieces, entry_at, place, arrays, maps_v, up_map, (m_sem, u_sem),
        lambda block, side: token_copy(block, side).start(),
    )
    sums[...] = priors[0][...] if priors else jnp.zeros_like(sums)
    add_maps(
        pieces, entry_at, place, maps_v, tokens_v, up_map, sums, (m_sem, u_sem),
        lambda block, side: token_copy(block, side).wait(),
    )


def shrink_sums(scalars, tokens, arrays, pieces, prior, hint):
    rows, width = tokens.shape
    blocks, count = rows // BLK, len(arrays)
    half = pieces[0][-1]
    return pl.pallas_call(
        functools.partial(shrink_kernel, pieces, count, len(prior)),
        in_specs=[SMEM, SMEM, SMEM] + [ANY] * (1 + count) + [VMEM, ANY][: len(prior)],
        out_specs=[VMEM, ANY],
        out_shape=[
            jax.ShapeDtypeStruct((blocks, ADAPTER_RANK, BLK), jnp.float32),
            jax.ShapeDtypeStruct((blocks, ADAPTER_RANK, 2 * half), jnp.bfloat16),
        ],
        input_output_aliases={5 + count: 1} if prior else {},
        scratch_shapes=[
            pltpu.VMEM((rows, width), tokens.dtype),
            pltpu.SemaphoreType.DMA((blocks, 2)),
        ]
        + map_scratch(blocks, width // 2, tokens.dtype),
        compiler_params=kernel_params(50),
        cost_estimate=hint,
    )(*scalars, tokens, *arrays, *prior)


def final_kernel(place, live, base, sums, far_sums, ups, keys):
    blocks, _, half = ups.shape
    for block in range(blocks):
        total = sums[block] + far_sums[block]
        high = total.astype(jnp.bfloat16)
        rest = total - high.astype(jnp.float32)
        middle = rest.astype(jnp.bfloat16)
        low = (rest - middle.astype(jnp.float32)).astype(jnp.bfloat16)
        up = ups[block]
        delta = lax.dot_general(
            jnp.concatenate([high, middle, low], axis=0),
            jnp.concatenate([up, up, up], axis=0),
            TN,
            preferred_element_type=jnp.float32,
        )
        row = lax.broadcasted_iota(jnp.int32, (BLK, half), 0)
        fill = live[place[1] * blocks + block]
        span = slice(block * BLK, (block + 1) * BLK)
        keys[span, :] = jnp.where(row < fill, base[span, :] + delta, 0.0).astype(keys.dtype)


def final_keys(place, live, base, sums, far_sums, ups):
    rows, half = base.shape
    return pl.pallas_call(
        final_kernel,
        in_specs=[SMEM, SMEM] + [VMEM] * 4,
        out_specs=VMEM,
        out_shape=jax.ShapeDtypeStruct((rows, half), jnp.bfloat16),
        compiler_params=kernel_params(12),
        cost_estimate=LIGHT,
    )(place, live, base, sums, far_sums, ups)


def per_device_planes(
    tokens,
    key_projection_weight,
    adapter_down_weight,
    adapter_up_weight,
    adapter_pool_index,
    block_adapter_index,
    block_live_tokens,
):
    place = jnp.stack(
        [lax.axis_index("groups"), lax.axis_index("dp"), lax.axis_index("tensor")]
    ).astype(jnp.int32)
    down, up = adapter_down_weight[0], adapter_up_weight[0]
    width, half = down.shape[1] // 2, up.shape[1] // 2
    piece = width + half
    own = jnp.concatenate([down[:, :width], up[:, :half], down[:, width:], up[:, half:]], axis=1)
    first = lax.axis_index("groups") == 0
    own_half = jnp.where(first, own[:, :piece], own[:, piece:])

    def ring(array, step):
        pairs = [(2 * z + y, 2 * ((z + step) % 4) + y) for z in range(4) for y in range(2)]
        return lax.ppermute(array, "dp", pairs)

    def over_y(array):
        return lax.ppermute(array, "dp", [(i, i ^ 1) for i in range(8)])

    def over_x(array):
        return lax.ppermute(array, "groups", SWAP)

    def over_cores(array):
        return lax.ppermute(array, "tensor", SWAP)

    scalars = (place, adapter_pool_index, block_adapter_index[:, 0])
    weight = key_projection_weight
    z1 = ring(own_half, 1)
    y0 = over_y(own)
    z3 = ring(own_half, -1)
    fars = base_sums(place, tokens, weight, True, FAR_PARTS, LIGHT)
    z1_ = after(z1, fars[0])
    x1 = over_x(z1_)
    y1 = over_y(z1_)
    z2a = ring(z1_, 1)
    z3_ = after(z3, z1_)
    x3 = over_x(z3_)
    y3 = over_y(after(z3_, y0))
    z2b = ring(x1, 1)
    y2a = over_y(z2a)
    x1y = over_x(y1)
    (mine,) = base_sums(place, after(tokens, x1, z2a, y1), weight, False, 1, HEAVY)
    x3y = over_x(y3)
    y2b = over_y(after(z2b, mine))

    def named(first, entries):
        return [
            (entry, kind, (first + at, 0), (first + at, width), half)
            for at, (entry, kind) in enumerate(entries)
        ]

    prior = shrink_sums(
        scalars,
        after(tokens, z2b, x1y, y2a, mine),
        [down, up, y0, z1, z3, x1, y1, z2a, x3, y3],
        [
            (0, "a", (0, 0), (1, 0), half),
            (0, "b", (0, width), (1, half), half),
            (1, "a", (2, 0), (2, width), half),
            (1, "b", (2, piece), (2, piece + width), half),
        ]
        + named(
            3,
            [(2, "own"), (6, "own"), (2, "far"), (3, "own"), (4, "own"), (6, "far"), (7, "own")],
        ),
        [],
        HEAVY,
    )
    base_fars = [over_cores(after(far, prior[0])) for far in fars]
    prior = shrink_sums(
        scalars,
        tokens,
        [z2b, x1y, x3y, y2a],
        named(0, [(4, "far"), (3, "far"), (7, "far"), (5, "own")]),
        prior,
        HEAVY,
    )
    base = mine + jnp.concatenate(base_fars, axis=0)
    sums, ups = shrink_sums(
        scalars, tokens, [y2b], named(0, [(5, "far")]), prior, LIGHT
    )
    far_sums = over_cores(sums)
    return final_keys(place, block_live_tokens, base, sums, far_sums, ups)


def per_device_gathered(
    tokens,
    key_projection_weight,
    adapter_down_weight,
    adapter_up_weight,
    adapter_pool_index,
    block_adapter_index,
    block_live_tokens,
):
    rows = tokens.shape[0]
    blocks = rows // BLK
    first_block = lax.axis_index("dp") * blocks
    slots = lax.dynamic_slice_in_dim(
        adapter_pool_index[block_adapter_index[:, 0]], first_block, blocks
    )
    fill = lax.dynamic_slice_in_dim(block_live_tokens, first_block, blocks)
    base_part = jnp.dot(tokens, key_projection_weight, preferred_element_type=jnp.float32)
    down = lax.all_gather(adapter_down_weight, "dp", axis=0, tiled=True)
    up = lax.all_gather(adapter_up_weight, "dp", axis=0, tiled=True)
    token_blocks = tokens.reshape(blocks, BLK, tokens.shape[1])
    shrink = jnp.einsum(
        "nrd,nbd->rnb",
        jnp.take(down, slots, axis=0),
        token_blocks,
        preferred_element_type=jnp.float32,
    )
    shrink = lax.psum(shrink.reshape(ADAPTER_RANK, rows), "tensor")
    delta = jnp.einsum(
        "rnb,nrc->nbc",
        shrink.reshape(ADAPTER_RANK, blocks, BLK),
        jnp.take(up, slots, axis=0).astype(jnp.float32),
        precision=lax.Precision.HIGHEST,
        preferred_element_type=jnp.float32,
    )
    base = lax.psum_scatter(base_part, "tensor", scatter_dimension=1, tiled=True)
    mask = jnp.arange(BLK, dtype=jnp.int32)[None, :] < fill[:, None]
    keys = base + delta.reshape(rows, base.shape[1])
    return jnp.where(mask.reshape(rows, 1), keys, 0.0).astype(jnp.bfloat16)


def solution(mesh):
    in_specs = (
        P(("groups", "dp"), "tensor"),
        P("tensor", None),
        P("dp", None, "tensor"),
        P("dp", None, "tensor"),
        P(),
        P("groups", None),
        P("groups"),
    )
    out_specs = P(("groups", "dp"), "tensor")
    planes = dict(mesh.shape) == {"groups": 2, "dp": 8, "tensor": 2}
    return jax.shard_map(
        per_device_planes if planes else per_device_gathered,
        mesh=mesh,
        in_specs=in_specs,
        out_specs=out_specs,
        check_vma=False,
    )
```

```python
import functools

import jax
import jax.numpy as jnp
from jax import lax
from jax.experimental import pallas as pl
from jax.experimental.pallas import tpu as pltpu
from jax.sharding import PartitionSpec as P

ADAPTER_RANK = 64
BLK = 128
FAR_PARTS = 3
SWAP = [(0, 1), (1, 0)]
NT = (((1,), (1,)), ((), ()))
TN = (((0,), (0,)), ((), ()))


def kernel_params(mebibytes):
    return pltpu.CompilerParams(vmem_limit_bytes=mebibytes * 1024 * 1024)


LIGHT = pl.CostEstimate(flops=1, bytes_accessed=1, transcendentals=0)
HEAVY = pl.CostEstimate(flops=30000000000, bytes_accessed=1, transcendentals=0)


def after(array, *others):
    return lax.optimization_barrier((array, *others))[0]


SMEM = pl.BlockSpec(memory_space=pltpu.SMEM)
VMEM = pl.BlockSpec(memory_space=pltpu.VMEM)
ANY = pl.BlockSpec(memory_space=pl.ANY)


def base_kernel(cuts, other, place, tokens, weight, *refs):
    core = 1 - place[2] if other else place[2]
    base_steps(cuts, core, tokens, weight, refs[:-4], refs[-4:])


def base_steps(cuts, core, tokens, weight, outs, scratch):
    tokens_v, weight_v, t_sem, w_sem = scratch
    part, half = outs[0].shape
    columns = pl.ds(pl.multiple_of(core * half, half), half)
    copies = []
    for step, (start, depth) in enumerate(cuts):
        span = pl.ds(start, depth)
        pair = (
            pltpu.make_async_copy(tokens.at[:, span], tokens_v.at[:, span], t_sem.at[step]),
            pltpu.make_async_copy(weight.at[span, columns], weight_v.at[span, :], w_sem.at[step]),
        )
        for copy in pair:
            copy.start()
        copies.append(pair)
    for step, (start, depth) in enumerate(cuts):
        for copy in copies[step]:
            copy.wait()
        for at, out in enumerate(outs):
            product = jnp.dot(
                tokens_v[pl.ds(at * part, part), pl.ds(start, depth)],
                weight_v[pl.ds(start, depth), :],
                preferred_element_type=jnp.float32,
            )
            out[...] = product if step == 0 else out[...] + product


def base_cuts(width):
    eighth = width // 8
    return [(0, eighth)] + [(at * eighth, 2 * eighth) for at in (1, 3, 5)] + [(7 * eighth, eighth)]


def base_scratch(tokens, weight):
    rows, width = tokens.shape
    steps = len(base_cuts(width))
    return [
        pltpu.VMEM((rows, width), tokens.dtype),
        pltpu.VMEM((width, weight.shape[1] // 2), weight.dtype),
        pltpu.SemaphoreType.DMA((steps,)),
        pltpu.SemaphoreType.DMA((steps,)),
    ]


def base_sums(place, tokens, weight, other, parts, hint):
    rows, width = tokens.shape
    half = weight.shape[1] // 2
    return pl.pallas_call(
        functools.partial(base_kernel, base_cuts(width), other),
        in_specs=[SMEM, ANY, ANY],
        out_specs=[VMEM] * parts,
        out_shape=[jax.ShapeDtypeStruct((rows // parts, half), jnp.float32)] * parts,
        scratch_shapes=base_scratch(tokens, weight),
        compiler_params=kernel_params(50),
        cost_estimate=hint,
    )(place, tokens, weight)


def entry_of(place, slot):
    back = ((place[1] >> 1) - (slot >> 1)) & 3
    return 2 * back + ((slot ^ place[1]) & 1)


def side_of(place, kind):
    return {"a": 0, "b": 1, "own": place[0], "far": 1 - place[0]}[kind]


def start_maps(pieces, entry_at, place, arrays, maps_v, up_map, sems, start_tokens):
    m_sem, u_sem = sems
    blocks, _, _, wide = maps_v.shape

    def start(block, carry):
        entry = entry_at(block)
        for at_entry, kind, (at, column), (up_at, up_column), half in pieces:

            @pl.when(entry == at_entry)
            def _(kind=kind, at=at, column=column, up_at=up_at, up_column=up_column):
                side = side_of(place, kind)
                start_tokens(block, side)
                pltpu.make_async_copy(
                    arrays[at].at[:, column : column + wide],
                    maps_v.at[block, side],
                    m_sem.at[block, side],
                ).start()
                pltpu.make_async_copy(
                    arrays[up_at].at[:, up_column : up_column + half],
                    up_map.at[block, :, pl.ds(pl.multiple_of(side * half, half), half)],
                    u_sem.at[block, side],
                ).start()

        return carry

    lax.fori_loop(0, blocks, start, 0)


def add_maps(pieces, entry_at, place, maps_v, tokens_v, up_map, sums, sems, wait_tokens):
    m_sem, u_sem = sems
    blocks, _, _, wide = maps_v.shape
    half = up_map.shape[2] // 2
    masks = []
    for side in range(2):
        bits = {"a": 0, "b": 0, "own": 0, "far": 0}
        for entry, kind, *_ in pieces:
            bits[kind] |= 1 << entry
        masks.append(
            bits["a" if side == 0 else "b"]
            | jnp.where(place[0] == side, bits["own"], bits["far"])
        )

    def add(block, carry):
        entry = entry_at(block)
        for side in range(2):

            @pl.when(((masks[side] >> entry) & 1) == 1)
            def _(side=side):
                wait_tokens(block, side)
                pltpu.make_async_copy(
                    maps_v.at[block, side], maps_v.at[block, side], m_sem.at[block, side]
                ).wait()
                sums[block] += lax.dot_general(
                    maps_v[block, side],
                    tokens_v[pl.ds(pl.multiple_of(block * BLK, BLK), BLK), pl.ds(side * wide, wide)],
                    NT,
                    preferred_element_type=jnp.float32,
                )
                half_map = up_map.at[block, :, pl.ds(side * half, half)]
                pltpu.make_async_copy(half_map, half_map, u_sem.at[block, side]).wait()

        return carry

    lax.fori_loop(0, blocks, add, 0)


def map_scratch(blocks, wide, dtype):
    return [
        pltpu.VMEM((blocks, 2, ADAPTER_RANK, wide), dtype),
        pltpu.SemaphoreType.DMA((blocks, 2)),
        pltpu.SemaphoreType.DMA((blocks, 2)),
    ]


def shrink_kernel(pieces, count, prior_count, place, pool_index, adapter_index, tokens, *refs):
    arrays, priors = refs[:count], refs[count : count + prior_count]
    sums, up_map, tokens_v, t_sem, maps_v, m_sem, u_sem = refs[count + prior_count :]
    blocks, wide = sums.shape[0], maps_v.shape[3]

    def entry_at(block):
        return entry_of(place, pool_index[adapter_index[place[1] * blocks + block]])

    def token_copy(block, side):
        place_of = (
            pl.ds(pl.multiple_of(block * BLK, BLK), BLK),
            pl.ds(pl.multiple_of(side * wide, wide), wide),
        )
        return pltpu.make_async_copy(
            tokens.at[place_of], tokens_v.at[place_of], t_sem.at[block, side]
        )

    start_maps(
        pieces, entry_at, place, arrays, maps_v, up_map, (m_sem, u_sem),
        lambda block, side: token_copy(block, side).start(),
    )
    sums[...] = priors[0][...] if priors else jnp.zeros_like(sums)
    add_maps(
        pieces, entry_at, place, maps_v, tokens_v, up_map, sums, (m_sem, u_sem),
        lambda block, side: token_copy(block, side).wait(),
    )


def shrink_sums(scalars, tokens, arrays, pieces, prior, hint):
    rows, width = tokens.shape
    blocks, count = rows // BLK, len(arrays)
    half = pieces[0][-1]
    return pl.pallas_call(
        functools.partial(shrink_kernel, pieces, count, len(prior)),
        in_specs=[SMEM, SMEM, SMEM] + [ANY] * (1 + count) + [VMEM, ANY][: len(prior)],
        out_specs=[VMEM, ANY],
        out_shape=[
            jax.ShapeDtypeStruct((blocks, ADAPTER_RANK, BLK), jnp.float32),
            jax.ShapeDtypeStruct((blocks, ADAPTER_RANK, 2 * half), jnp.bfloat16),
        ],
        input_output_aliases={5 + count: 1} if prior else {},
        scratch_shapes=[
            pltpu.VMEM((rows, width), tokens.dtype),
            pltpu.SemaphoreType.DMA((blocks, 2)),
        ]
        + map_scratch(blocks, width // 2, tokens.dtype),
        compiler_params=kernel_params(50),
        cost_estimate=hint,
    )(*scalars, tokens, *arrays, *prior)


def final_kernel(place, live, base, sums, far_sums, ups, keys):
    blocks, _, half = ups.shape
    for block in range(blocks):
        total = sums[block] + far_sums[block]
        high = total.astype(jnp.bfloat16)
        rest = total - high.astype(jnp.float32)
        middle = rest.astype(jnp.bfloat16)
        low = (rest - middle.astype(jnp.float32)).astype(jnp.bfloat16)
        up = ups[block]
        delta = lax.dot_general(
            jnp.concatenate([high, middle, low], axis=0),
            jnp.concatenate([up, up, up], axis=0),
            TN,
            preferred_element_type=jnp.float32,
        )
        row = lax.broadcasted_iota(jnp.int32, (BLK, half), 0)
        fill = live[place[1] * blocks + block]
        span = slice(block * BLK, (block + 1) * BLK)
        keys[span, :] = jnp.where(row < fill, base[span, :] + delta, 0.0).astype(keys.dtype)


def final_keys(place, live, base, sums, far_sums, ups):
    rows, half = base.shape
    return pl.pallas_call(
        final_kernel,
        in_specs=[SMEM, SMEM] + [VMEM] * 4,
        out_specs=VMEM,
        out_shape=jax.ShapeDtypeStruct((rows, half), jnp.bfloat16),
        compiler_params=kernel_params(12),
        cost_estimate=LIGHT,
    )(place, live, base, sums, far_sums, ups)


def per_device_planes(
    tokens,
    key_projection_weight,
    adapter_down_weight,
    adapter_up_weight,
    adapter_pool_index,
    block_adapter_index,
    block_live_tokens,
):
    place = jnp.stack(
        [lax.axis_index("groups"), lax.axis_index("dp"), lax.axis_index("tensor")]
    ).astype(jnp.int32)
    down, up = adapter_down_weight[0], adapter_up_weight[0]
    width, half = down.shape[1] // 2, up.shape[1] // 2
    piece = width + half
    own = jnp.concatenate([down[:, :width], up[:, :half], down[:, width:], up[:, half:]], axis=1)
    first = lax.axis_index("groups") == 0
    own_half = jnp.where(first, own[:, :piece], own[:, piece:])

    def ring(array, step):
        pairs = [(2 * z + y, 2 * ((z + step) % 4) + y) for z in range(4) for y in range(2)]
        return lax.ppermute(array, "dp", pairs)

    def over_y(array):
        return lax.ppermute(array, "dp", [(i, i ^ 1) for i in range(8)])

    def over_x(array):
        return lax.ppermute(array, "groups", SWAP)

    def over_cores(array):
        return lax.ppermute(array, "tensor", SWAP)

    scalars = (place, adapter_pool_index, block_adapter_index[:, 0])
    weight = key_projection_weight
    z1 = ring(own_half, 1)
    y0 = over_y(own)
    z3 = ring(own_half, -1)
    fars = base_sums(place, tokens, weight, True, FAR_PARTS, LIGHT)
    z1_ = after(z1, fars[0])
    x1 = over_x(z1_)
    y1 = over_y(z1_)
    z3_ = after(z3, z1_)
    z2a = ring(after(z1_, z3), 1)
    x3 = over_x(z3_)
    y3 = over_y(after(z3_, y0))
    z2b = ring(x1, 1)
    y2a = over_y(z2a)
    x1y = over_x(y1)

    (mine,) = base_sums(place, after(tokens, z3_, y0), weight, False, 1, HEAVY)
    def named(first, entries):
        return [
            (entry, kind, (first + at, 0), (first + at, width), half)
            for at, (entry, kind) in enumerate(entries)
        ]

    prior = shrink_sums(
        scalars,
        after(tokens, mine, x1, y1, z2a),
        [down, up, y0, z1, z3],
        [
            (0, "a", (0, 0), (1, 0), half),
            (0, "b", (0, width), (1, half), half),
            (1, "a", (2, 0), (2, width), half),
            (1, "b", (2, piece), (2, piece + width), half),
        ]
        + named(3, [(2, "own"), (6, "own")]),
        [],
        HEAVY,
    )
    x3y = over_x(y3)
    y2b = over_y(after(z2b, prior[0]))
    prior = shrink_sums(
        scalars,
        after(tokens, z2b),
        [x1, y1, z2a, x3, y3],
        named(0, [(2, "far"), (3, "own"), (4, "own"), (6, "far"), (7, "own")]),
        prior,
        LIGHT,
    )
    base_fars = [over_cores(after(far, prior[0])) for far in fars]
    prior = shrink_sums(
        scalars,
        tokens,
        [z2b, x1y, x3y, y2a],
        named(0, [(4, "far"), (3, "far"), (7, "far"), (5, "own")]),
        prior,
        HEAVY,
    )
    base = mine + jnp.concatenate(base_fars, axis=0)
    sums, ups = shrink_sums(
        scalars, tokens, [y2b], named(0, [(5, "far")]), prior, LIGHT
    )
    far_sums = over_cores(sums)
    return final_keys(place, block_live_tokens, base, sums, far_sums, ups)


def per_device_gathered(
    tokens,
    key_projection_weight,
    adapter_down_weight,
    adapter_up_weight,
    adapter_pool_index,
    block_adapter_index,
    block_live_tokens,
):
    rows = tokens.shape[0]
    blocks = rows // BLK
    first_block = lax.axis_index("dp") * blocks
    slots = lax.dynamic_slice_in_dim(
        adapter_pool_index[block_adapter_index[:, 0]], first_block, blocks
    )
    fill = lax.dynamic_slice_in_dim(block_live_tokens, first_block, blocks)
    base_part = jnp.dot(tokens, key_projection_weight, preferred_element_type=jnp.float32)
    down = lax.all_gather(adapter_down_weight, "dp", axis=0, tiled=True)
    up = lax.all_gather(adapter_up_weight, "dp", axis=0, tiled=True)
    token_blocks = tokens.reshape(blocks, BLK, tokens.shape[1])
    shrink = jnp.einsum(
        "nrd,nbd->rnb",
        jnp.take(down, slots, axis=0),
        token_blocks,
        preferred_element_type=jnp.float32,
    )
    shrink = lax.psum(shrink.reshape(ADAPTER_RANK, rows), "tensor")
    delta = jnp.einsum(
        "rnb,nrc->nbc",
        shrink.reshape(ADAPTER_RANK, blocks, BLK),
        jnp.take(up, slots, axis=0).astype(jnp.float32),
        precision=lax.Precision.HIGHEST,
        preferred_element_type=jnp.float32,
    )
    base = lax.psum_scatter(base_part, "tensor", scatter_dimension=1, tiled=True)
    mask = jnp.arange(BLK, dtype=jnp.int32)[None, :] < fill[:, None]
    keys = base + delta.reshape(rows, base.shape[1])
    return jnp.where(mask.reshape(rows, 1), keys, 0.0).astype(jnp.bfloat16)


def solution(mesh):
    in_specs = (
        P(("groups", "dp"), "tensor"),
        P("tensor", None),
        P("dp", None, "tensor"),
        P("dp", None, "tensor"),
        P(),
        P("groups", None),
        P("groups"),
    )
    out_specs = P(("groups", "dp"), "tensor")
    planes = dict(mesh.shape) == {"groups": 2, "dp": 8, "tensor": 2}
    return jax.shard_map(
        per_device_planes if planes else per_device_gathered,
        mesh=mesh,
        in_specs=in_specs,
        out_specs=out_specs,
        check_vma=False,
    )
```

```python
import functools

import jax
import jax.numpy as jnp
from jax import lax
from jax.experimental import pallas as pl
from jax.experimental.pallas import tpu as pltpu
from jax.sharding import PartitionSpec as P

ADAPTER_RANK = 64
BLK = 128
FAR_PARTS = 3
SWAP = [(0, 1), (1, 0)]
NT = (((1,), (1,)), ((), ()))
TN = (((0,), (0,)), ((), ()))


def kernel_params(mebibytes):
    return pltpu.CompilerParams(vmem_limit_bytes=mebibytes * 1024 * 1024)


LIGHT = pl.CostEstimate(flops=1, bytes_accessed=1, transcendentals=0)
HEAVY = pl.CostEstimate(flops=30000000000, bytes_accessed=1, transcendentals=0)


def after(array, *others):
    return lax.optimization_barrier((array, *others))[0]


SMEM = pl.BlockSpec(memory_space=pltpu.SMEM)
VMEM = pl.BlockSpec(memory_space=pltpu.VMEM)
ANY = pl.BlockSpec(memory_space=pl.ANY)


def pack_kernel(place, down, up, own, own_half, sems):
    width, half = down.shape[1] // 2, up.shape[1] // 2
    piece = width + half

    def copies(side, out, column, at):
        down_span = pl.ds(pl.multiple_of(side * width, width), width)
        up_span = pl.ds(pl.multiple_of(side * half, half), half)
        return [
            pltpu.make_async_copy(
                down.at[:, down_span], out.at[:, pl.ds(column, width)], sems.at[at]
            ),
            pltpu.make_async_copy(
                up.at[:, up_span], out.at[:, pl.ds(column + width, half)], sems.at[at + 1]
            ),
        ]

    every = copies(0, own, 0, 0) + copies(1, own, piece, 2) + copies(place[0], own_half, 0, 4)
    for copy in every:
        copy.start()
    for copy in every:
        copy.wait()


def pack_own(place, down, up):
    rank, total = down.shape[0], down.shape[1] + up.shape[1]
    return pl.pallas_call(
        pack_kernel,
        in_specs=[SMEM, ANY, ANY],
        out_specs=[ANY, ANY],
        out_shape=[
            jax.ShapeDtypeStruct((rank, total), down.dtype),
            jax.ShapeDtypeStruct((rank, total // 2), down.dtype),
        ],
        scratch_shapes=[pltpu.SemaphoreType.DMA((6,))],
        compiler_params=kernel_params(58),
        cost_estimate=LIGHT,
    )(place, down, up)


def base_kernel(cuts, other, place, tokens, weight, *refs):
    core = 1 - place[2] if other else place[2]
    base_steps(cuts, core, tokens, weight, refs[:-4], refs[-4:])


def base_steps(cuts, core, tokens, weight, outs, scratch):
    tokens_v, weight_v, t_sem, w_sem = scratch
    part, half = outs[0].shape
    columns = pl.ds(pl.multiple_of(core * half, half), half)
    copies = []
    for step, (start, depth) in enumerate(cuts):
        span = pl.ds(start, depth)
        pair = (
            pltpu.make_async_copy(tokens.at[:, span], tokens_v.at[:, span], t_sem.at[step]),
            pltpu.make_async_copy(weight.at[span, columns], weight_v.at[span, :], w_sem.at[step]),
        )
        for copy in pair:
            copy.start()
        copies.append(pair)
    for step, (start, depth) in enumerate(cuts):
        for copy in copies[step]:
            copy.wait()
        for at, out in enumerate(outs):
            product = jnp.dot(
                tokens_v[pl.ds(at * part, part), pl.ds(start, depth)],
                weight_v[pl.ds(start, depth), :],
                preferred_element_type=jnp.float32,
            )
            out[...] = product if step == 0 else out[...] + product


def base_cuts(width):
    eighth = width // 8
    return [(0, eighth)] + [(at * eighth, 2 * eighth) for at in (1, 3, 5)] + [(7 * eighth, eighth)]


def base_scratch(tokens, weight):
    rows, width = tokens.shape
    steps = len(base_cuts(width))
    return [
        pltpu.VMEM((rows, width), tokens.dtype),
        pltpu.VMEM((width, weight.shape[1] // 2), weight.dtype),
        pltpu.SemaphoreType.DMA((steps,)),
        pltpu.SemaphoreType.DMA((steps,)),
    ]


def base_sums(place, tokens, weight, other, parts, hint):
    rows, width = tokens.shape
    half = weight.shape[1] // 2
    return pl.pallas_call(
        functools.partial(base_kernel, base_cuts(width), other),
        in_specs=[SMEM, ANY, ANY],
        out_specs=[VMEM] * parts,
        out_shape=[jax.ShapeDtypeStruct((rows // parts, half), jnp.float32)] * parts,
        scratch_shapes=base_scratch(tokens, weight),
        compiler_params=kernel_params(50),
        cost_estimate=hint,
    )(place, tokens, weight)


def entry_of(place, slot):
    back = ((place[1] >> 1) - (slot >> 1)) & 3
    return 2 * back + ((slot ^ place[1]) & 1)


def side_of(place, kind):
    return {"a": 0, "b": 1, "own": place[0], "far": 1 - place[0]}[kind]


def start_maps(pieces, entry_at, place, arrays, maps_v, up_map, sems, start_tokens):
    m_sem, u_sem = sems
    blocks, _, _, wide = maps_v.shape

    def start(block, carry):
        entry = entry_at(block)
        for at_entry, kind, (at, column), (up_at, up_column), half in pieces:

            @pl.when(entry == at_entry)
            def _(kind=kind, at=at, column=column, up_at=up_at, up_column=up_column):
                side = side_of(place, kind)
                start_tokens(block, side)
                pltpu.make_async_copy(
                    arrays[at].at[:, column : column + wide],
                    maps_v.at[block, side],
                    m_sem.at[block, side],
                ).start()
                pltpu.make_async_copy(
                    arrays[up_at].at[:, up_column : up_column + half],
                    up_map.at[block, :, pl.ds(pl.multiple_of(side * half, half), half)],
                    u_sem.at[block, side],
                ).start()

        return carry

    lax.fori_loop(0, blocks, start, 0)


def add_maps(pieces, entry_at, place, maps_v, tokens_v, up_map, sums, sems, wait_tokens):
    m_sem, u_sem = sems
    blocks, _, _, wide = maps_v.shape
    half = up_map.shape[2] // 2
    masks = []
    for side in range(2):
        bits = {"a": 0, "b": 0, "own": 0, "far": 0}
        for entry, kind, *_ in pieces:
            bits[kind] |= 1 << entry
        masks.append(
            bits["a" if side == 0 else "b"]
            | jnp.where(place[0] == side, bits["own"], bits["far"])
        )

    def add(block, carry):
        entry = entry_at(block)
        for side in range(2):

            @pl.when(((masks[side] >> entry) & 1) == 1)
            def _(side=side):
                wait_tokens(block, side)
                pltpu.make_async_copy(
                    maps_v.at[block, side], maps_v.at[block, side], m_sem.at[block, side]
                ).wait()
                sums[block] += lax.dot_general(
                    maps_v[block, side],
                    tokens_v[pl.ds(pl.multiple_of(block * BLK, BLK), BLK), pl.ds(side * wide, wide)],
                    NT,
                    preferred_element_type=jnp.float32,
                )
                half_map = up_map.at[block, :, pl.ds(side * half, half)]
                pltpu.make_async_copy(half_map, half_map, u_sem.at[block, side]).wait()

        return carry

    lax.fori_loop(0, blocks, add, 0)


def map_scratch(blocks, wide, dtype):
    return [
        pltpu.VMEM((blocks, 2, ADAPTER_RANK, wide), dtype),
        pltpu.SemaphoreType.DMA((blocks, 2)),
        pltpu.SemaphoreType.DMA((blocks, 2)),
    ]


def shrink_kernel(pieces, count, prior_count, place, pool_index, adapter_index, tokens, *refs):
    arrays, priors = refs[:count], refs[count : count + prior_count]
    sums, up_map, tokens_v, t_sem, maps_v, m_sem, u_sem = refs[count + prior_count :]
    blocks, wide = sums.shape[0], maps_v.shape[3]

    def entry_at(block):
        return entry_of(place, pool_index[adapter_index[place[1] * blocks + block]])

    def token_copy(block, side):
        place_of = (
            pl.ds(pl.multiple_of(block * BLK, BLK), BLK),
            pl.ds(pl.multiple_of(side * wide, wide), wide),
        )
        return pltpu.make_async_copy(
            tokens.at[place_of], tokens_v.at[place_of], t_sem.at[block, side]
        )

    start_maps(
        pieces, entry_at, place, arrays, maps_v, up_map, (m_sem, u_sem),
        lambda block, side: token_copy(block, side).start(),
    )
    sums[...] = priors[0][...] if priors else jnp.zeros_like(sums)
    add_maps(
        pieces, entry_at, place, maps_v, tokens_v, up_map, sums, (m_sem, u_sem),
        lambda block, side: token_copy(block, side).wait(),
    )


def shrink_sums(scalars, tokens, arrays, pieces, prior, hint):
    rows, width = tokens.shape
    blocks, count = rows // BLK, len(arrays)
    half = pieces[0][-1]
    return pl.pallas_call(
        functools.partial(shrink_kernel, pieces, count, len(prior)),
        in_specs=[SMEM, SMEM, SMEM] + [ANY] * (1 + count) + [VMEM, ANY][: len(prior)],
        out_specs=[VMEM, ANY],
        out_shape=[
            jax.ShapeDtypeStruct((blocks, ADAPTER_RANK, BLK), jnp.float32),
            jax.ShapeDtypeStruct((blocks, ADAPTER_RANK, 2 * half), jnp.bfloat16),
        ],
        input_output_aliases={5 + count: 1} if prior else {},
        scratch_shapes=[
            pltpu.VMEM((rows, width), tokens.dtype),
            pltpu.SemaphoreType.DMA((blocks, 2)),
        ]
        + map_scratch(blocks, width // 2, tokens.dtype),
        compiler_params=kernel_params(50),
        cost_estimate=hint,
    )(*scalars, tokens, *arrays, *prior)


def final_kernel(place, live, base, sums, far_sums, ups, keys, base_v, keys_v, in_sem, out_sem):
    blocks, _, half = ups.shape

    def rows_of(block):
        return pl.ds(block * BLK, BLK)

    def load(block):
        rows = rows_of(block)
        return pltpu.make_async_copy(base.at[rows, :], base_v.at[rows, :], in_sem.at[block])

    def store(block):
        rows = rows_of(block)
        return pltpu.make_async_copy(keys_v.at[rows, :], keys.at[rows, :], out_sem.at[block])

    for block in range(blocks):
        load(block).start()
    for block in range(blocks):
        total = sums[block] + far_sums[block]
        high = total.astype(jnp.bfloat16)
        rest = total - high.astype(jnp.float32)
        middle = rest.astype(jnp.bfloat16)
        low = (rest - middle.astype(jnp.float32)).astype(jnp.bfloat16)
        up = ups[block]
        delta = lax.dot_general(
            jnp.concatenate([high, middle, low], axis=0),
            jnp.concatenate([up, up, up], axis=0),
            TN,
            preferred_element_type=jnp.float32,
        )
        load(block).wait()
        row = lax.broadcasted_iota(jnp.int32, (BLK, half), 0)
        fill = live[place[1] * blocks + block]
        rows = rows_of(block)
        keys_v[rows, :] = jnp.where(row < fill, base_v[rows, :] + delta, 0.0).astype(keys.dtype)
        store(block).start()
    for block in range(blocks):
        store(block).wait()


def final_keys(place, live, base, sums, far_sums, ups):
    rows, half = base.shape
    blocks = rows // BLK
    return pl.pallas_call(
        final_kernel,
        in_specs=[SMEM, SMEM, ANY, VMEM, VMEM, VMEM],
        out_specs=ANY,
        out_shape=jax.ShapeDtypeStruct((rows, half), jnp.bfloat16),
        scratch_shapes=[
            pltpu.VMEM((rows, half), base.dtype),
            pltpu.VMEM((rows, half), jnp.bfloat16),
            pltpu.SemaphoreType.DMA((blocks,)),
            pltpu.SemaphoreType.DMA((blocks,)),
        ],
        compiler_params=kernel_params(12),
        cost_estimate=LIGHT,
    )(place, live, base, sums, far_sums, ups)


def per_device_planes(
    tokens,
    key_projection_weight,
    adapter_down_weight,
    adapter_up_weight,
    adapter_pool_index,
    block_adapter_index,
    block_live_tokens,
):
    place = jnp.stack(
        [lax.axis_index("groups"), lax.axis_index("dp"), lax.axis_index("tensor")]
    ).astype(jnp.int32)
    down, up = adapter_down_weight[0], adapter_up_weight[0]
    width, half = down.shape[1] // 2, up.shape[1] // 2
    piece = width + half
    own, own_half = pack_own(place, down, up)

    def ring(array, step):
        pairs = [(2 * z + y, 2 * ((z + step) % 4) + y) for z in range(4) for y in range(2)]
        return lax.ppermute(array, "dp", pairs)

    def over_y(array):
        return lax.ppermute(array, "dp", [(i, i ^ 1) for i in range(8)])

    def over_x(array):
        return lax.ppermute(array, "groups", SWAP)

    def over_cores(array):
        return lax.ppermute(array, "tensor", SWAP)

    scalars = (place, adapter_pool_index, block_adapter_index[:, 0])
    weight = key_projection_weight
    z1 = ring(own_half, 1)
    y0 = over_y(own)
    z3 = ring(own_half, -1)
    fars = base_sums(place, tokens, weight, True, FAR_PARTS, LIGHT)
    z1_ = after(z1, fars[0])
    x1 = over_x(z1_)
    y1 = over_y(z1_)
    z3_ = after(z3, z1_)
    z2a = ring(after(z1_, z3), 1)
    x3 = over_x(z3_)
    y3 = over_y(after(z3_, y0))
    z2b = ring(x1, 1)
    y2a = over_y(z2a)
    x1y = over_x(y1)

    (mine,) = base_sums(place, after(tokens, z3_, y0), weight, False, 1, HEAVY)
    def named(first, entries):
        return [
            (entry, kind, (first + at, 0), (first + at, width), half)
            for at, (entry, kind) in enumerate(entries)
        ]

    prior = shrink_sums(
        scalars,
        after(tokens, mine, x1, y1, z2a),
        [down, up, y0, z1, z3],
        [
            (0, "a", (0, 0), (1, 0), half),
            (0, "b", (0, width), (1, half), half),
            (1, "a", (2, 0), (2, width), half),
            (1, "b", (2, piece), (2, piece + width), half),
        ]
        + named(3, [(2, "own"), (6, "own")]),
        [],
        HEAVY,
    )
    x3y = over_x(y3)
    y2b = over_y(after(z2b, prior[0]))
    prior = shrink_sums(
        scalars,
        after(tokens, z2b),
        [x1, y1, z2a, x3, y3],
        named(0, [(2, "far"), (3, "own"), (4, "own"), (6, "far"), (7, "own")]),
        prior,
        LIGHT,
    )
    base_fars = [over_cores(after(far, prior[0])) for far in fars]
    prior = shrink_sums(
        scalars,
        tokens,
        [z2b, x1y, x3y, y2a],
        named(0, [(4, "far"), (3, "far"), (7, "far"), (5, "own")]),
        prior,
        HEAVY,
    )
    base = mine + jnp.concatenate(base_fars, axis=0)
    sums, ups = shrink_sums(
        scalars, tokens, [y2b], named(0, [(5, "far")]), prior, LIGHT
    )
    far_sums = over_cores(sums)
    return final_keys(place, block_live_tokens, base, sums, far_sums, ups)


def per_device_gathered(
    tokens,
    key_projection_weight,
    adapter_down_weight,
    adapter_up_weight,
    adapter_pool_index,
    block_adapter_index,
    block_live_tokens,
):
    rows = tokens.shape[0]
    blocks = rows // BLK
    first_block = lax.axis_index("dp") * blocks
    slots = lax.dynamic_slice_in_dim(
        adapter_pool_index[block_adapter_index[:, 0]], first_block, blocks
    )
    fill = lax.dynamic_slice_in_dim(block_live_tokens, first_block, blocks)
    base_part = jnp.dot(tokens, key_projection_weight, preferred_element_type=jnp.float32)
    down = lax.all_gather(adapter_down_weight, "dp", axis=0, tiled=True)
    up = lax.all_gather(adapter_up_weight, "dp", axis=0, tiled=True)
    token_blocks = tokens.reshape(blocks, BLK, tokens.shape[1])
    shrink = jnp.einsum(
        "nrd,nbd->rnb",
        jnp.take(down, slots, axis=0),
        token_blocks,
        preferred_element_type=jnp.float32,
    )
    shrink = lax.psum(shrink.reshape(ADAPTER_RANK, rows), "tensor")
    delta = jnp.einsum(
        "rnb,nrc->nbc",
        shrink.reshape(ADAPTER_RANK, blocks, BLK),
        jnp.take(up, slots, axis=0).astype(jnp.float32),
        precision=lax.Precision.HIGHEST,
        preferred_element_type=jnp.float32,
    )
    base = lax.psum_scatter(base_part, "tensor", scatter_dimension=1, tiled=True)
    mask = jnp.arange(BLK, dtype=jnp.int32)[None, :] < fill[:, None]
    keys = base + delta.reshape(rows, base.shape[1])
    return jnp.where(mask.reshape(rows, 1), keys, 0.0).astype(jnp.bfloat16)


def solution(mesh):
    in_specs = (
        P(("groups", "dp"), "tensor"),
        P("tensor", None),
        P("dp", None, "tensor"),
        P("dp", None, "tensor"),
        P(),
        P("groups", None),
        P("groups"),
    )
    out_specs = P(("groups", "dp"), "tensor")
    planes = dict(mesh.shape) == {"groups": 2, "dp": 8, "tensor": 2}
    return jax.shard_map(
        per_device_planes if planes else per_device_gathered,
        mesh=mesh,
        in_specs=in_specs,
        out_specs=out_specs,
        check_vma=False,
    )
```

```python
import functools

import jax
import jax.numpy as jnp
from jax import lax
from jax.experimental import pallas as pl
from jax.experimental.pallas import tpu as pltpu
from jax.sharding import PartitionSpec as P

ADAPTER_RANK = 64
BLK = 128
FAR_PARTS = 3
SWAP = [(0, 1), (1, 0)]
NT = (((1,), (1,)), ((), ()))
TN = (((0,), (0,)), ((), ()))


def kernel_params(mebibytes):
    return pltpu.CompilerParams(vmem_limit_bytes=mebibytes * 1024 * 1024)


LIGHT = pl.CostEstimate(flops=1, bytes_accessed=1, transcendentals=0)
HEAVY = pl.CostEstimate(flops=30000000000, bytes_accessed=1, transcendentals=0)


def after(array, *others):
    return lax.optimization_barrier((array, *others))[0]


SMEM = pl.BlockSpec(memory_space=pltpu.SMEM)
VMEM = pl.BlockSpec(memory_space=pltpu.VMEM)
ANY = pl.BlockSpec(memory_space=pl.ANY)


def base_kernel(cuts, runs, half, place, tokens, weight, *refs):
    outs, (tokens_v, weight_v, t_sem, w_sem) = list(refs[:-4]), refs[-4:]
    copies, first = [], 0
    for step, (start, depth) in enumerate(cuts):
        span = pl.ds(start, depth)
        copies.append(
            [pltpu.make_async_copy(tokens.at[:, span], tokens_v.at[:, span], t_sem.at[step])]
        )
        first = 0
        for at, (other, column, count, _) in enumerate(runs):
            core = 1 - place[2] if other else place[2]
            columns = pl.ds(pl.multiple_of(core * half + column, count), count)
            copies[-1].append(
                pltpu.make_async_copy(
                    weight.at[span, columns],
                    weight_v.at[span, pl.ds(first, count)],
                    w_sem.at[step, at],
                )
            )
            first += count
        for copy in copies[-1]:
            copy.start()
    for step, (start, depth) in enumerate(cuts):
        for copy in copies[step]:
            copy.wait()
        first, place_of = 0, 0
        for _, _, count, parts in runs:
            for at in range(parts):
                out = outs[place_of + at]
                part = out.shape[0]
                product = jnp.dot(
                    tokens_v[pl.ds(at * part, part), pl.ds(start, depth)],
                    weight_v[pl.ds(start, depth), pl.ds(first, count)],
                    preferred_element_type=jnp.float32,
                )
                out[...] = product if step == 0 else out[...] + product
            first += count
            place_of += parts


def base_cuts(width):
    eighth = width // 8
    return [(0, eighth)] + [(at * eighth, 2 * eighth) for at in (1, 3, 5)] + [(7 * eighth, eighth)]


def base_sums(place, tokens, weight, runs, hint):
    rows, width = tokens.shape
    steps = len(base_cuts(width))
    shapes = [
        jax.ShapeDtypeStruct((rows // parts, count), jnp.float32)
        for _, _, count, parts in runs
        for _ in range(parts)
    ]
    return pl.pallas_call(
        functools.partial(base_kernel, base_cuts(width), runs, weight.shape[1] // 2),
        in_specs=[SMEM, ANY, ANY],
        out_specs=[VMEM] * len(shapes),
        out_shape=shapes,
        scratch_shapes=[
            pltpu.VMEM((rows, width), tokens.dtype),
            pltpu.VMEM((width, sum(count for _, _, count, _ in runs)), weight.dtype),
            pltpu.SemaphoreType.DMA((steps,)),
            pltpu.SemaphoreType.DMA((steps, len(runs))),
        ],
        compiler_params=kernel_params(50),
        cost_estimate=hint,
    )(place, tokens, weight)


def entry_of(place, slot):
    back = ((place[1] >> 1) - (slot >> 1)) & 3
    return 2 * back + ((slot ^ place[1]) & 1)


def side_of(place, kind):
    return {"a": 0, "b": 1, "own": place[0], "far": 1 - place[0]}[kind]


def start_maps(pieces, entry_at, place, arrays, maps_v, up_map, sems, start_tokens):
    m_sem, u_sem = sems
    blocks, _, _, wide = maps_v.shape

    def start(block, carry):
        entry = entry_at(block)
        for at_entry, kind, (at, column), (up_at, up_column), half in pieces:

            @pl.when(entry == at_entry)
            def _(kind=kind, at=at, column=column, up_at=up_at, up_column=up_column):
                side = side_of(place, kind)
                start_tokens(block, side)
                pltpu.make_async_copy(
                    arrays[at].at[:, column : column + wide],
                    maps_v.at[block, side],
                    m_sem.at[block, side],
                ).start()
                pltpu.make_async_copy(
                    arrays[up_at].at[:, up_column : up_column + half],
                    up_map.at[block, :, pl.ds(pl.multiple_of(side * half, half), half)],
                    u_sem.at[block, side],
                ).start()

        return carry

    lax.fori_loop(0, blocks, start, 0)


def add_maps(pieces, entry_at, place, maps_v, tokens_v, up_map, sums, sems, wait_tokens):
    m_sem, u_sem = sems
    blocks, _, _, wide = maps_v.shape
    half = up_map.shape[2] // 2
    masks = []
    for side in range(2):
        bits = {"a": 0, "b": 0, "own": 0, "far": 0}
        for entry, kind, *_ in pieces:
            bits[kind] |= 1 << entry
        masks.append(
            bits["a" if side == 0 else "b"]
            | jnp.where(place[0] == side, bits["own"], bits["far"])
        )

    def add(block, carry):
        entry = entry_at(block)
        for side in range(2):

            @pl.when(((masks[side] >> entry) & 1) == 1)
            def _(side=side):
                wait_tokens(block, side)
                pltpu.make_async_copy(
                    maps_v.at[block, side], maps_v.at[block, side], m_sem.at[block, side]
                ).wait()
                sums[block] += lax.dot_general(
                    maps_v[block, side],
                    tokens_v[pl.ds(pl.multiple_of(block * BLK, BLK), BLK), pl.ds(side * wide, wide)],
                    NT,
                    preferred_element_type=jnp.float32,
                )
                half_map = up_map.at[block, :, pl.ds(side * half, half)]
                pltpu.make_async_copy(half_map, half_map, u_sem.at[block, side]).wait()

        return carry

    lax.fori_loop(0, blocks, add, 0)


def map_scratch(blocks, wide, dtype):
    return [
        pltpu.VMEM((blocks, 2, ADAPTER_RANK, wide), dtype),
        pltpu.SemaphoreType.DMA((blocks, 2)),
        pltpu.SemaphoreType.DMA((blocks, 2)),
    ]


def shrink_kernel(pieces, count, prior_count, place, pool_index, adapter_index, tokens, *refs):
    arrays, priors = refs[:count], refs[count : count + prior_count]
    sums, up_map, tokens_v, t_sem, maps_v, m_sem, u_sem = refs[count + prior_count :]
    blocks, wide = sums.shape[0], maps_v.shape[3]

    def entry_at(block):
        return entry_of(place, pool_index[adapter_index[place[1] * blocks + block]])

    def token_copy(block, side):
        place_of = (
            pl.ds(pl.multiple_of(block * BLK, BLK), BLK),
            pl.ds(pl.multiple_of(side * wide, wide), wide),
        )
        return pltpu.make_async_copy(
            tokens.at[place_of], tokens_v.at[place_of], t_sem.at[block, side]
        )

    start_maps(
        pieces, entry_at, place, arrays, maps_v, up_map, (m_sem, u_sem),
        lambda block, side: token_copy(block, side).start(),
    )
    sums[...] = priors[0][...] if priors else jnp.zeros_like(sums)
    add_maps(
        pieces, entry_at, place, maps_v, tokens_v, up_map, sums, (m_sem, u_sem),
        lambda block, side: token_copy(block, side).wait(),
    )


def shrink_sums(scalars, tokens, arrays, pieces, prior, hint):
    rows, width = tokens.shape
    blocks, count = rows // BLK, len(arrays)
    half = pieces[0][-1]
    return pl.pallas_call(
        functools.partial(shrink_kernel, pieces, count, len(prior)),
        in_specs=[SMEM, SMEM, SMEM] + [ANY] * (1 + count) + [VMEM, ANY][: len(prior)],
        out_specs=[VMEM, ANY],
        out_shape=[
            jax.ShapeDtypeStruct((blocks, ADAPTER_RANK, BLK), jnp.float32),
            jax.ShapeDtypeStruct((blocks, ADAPTER_RANK, 2 * half), jnp.bfloat16),
        ],
        input_output_aliases={5 + count: 1} if prior else {},
        scratch_shapes=[
            pltpu.VMEM((rows, width), tokens.dtype),
            pltpu.SemaphoreType.DMA((blocks, 2)),
        ]
        + map_scratch(blocks, width // 2, tokens.dtype),
        compiler_params=kernel_params(50),
        cost_estimate=hint,
    )(*scalars, tokens, *arrays, *prior)


def final_kernel(place, live, base, sums, far_sums, ups, keys):
    blocks, _, half = ups.shape
    for block in range(blocks):
        total = sums[block] + far_sums[block]
        high = total.astype(jnp.bfloat16)
        rest = total - high.astype(jnp.float32)
        middle = rest.astype(jnp.bfloat16)
        low = (rest - middle.astype(jnp.float32)).astype(jnp.bfloat16)
        up = ups[block]
        delta = lax.dot_general(
            jnp.concatenate([high, middle, low], axis=0),
            jnp.concatenate([up, up, up], axis=0),
            TN,
            preferred_element_type=jnp.float32,
        )
        row = lax.broadcasted_iota(jnp.int32, (BLK, half), 0)
        fill = live[place[1] * blocks + block]
        span = slice(block * BLK, (block + 1) * BLK)
        keys[span, :] = jnp.where(row < fill, base[span, :] + delta, 0.0).astype(keys.dtype)


def final_keys(place, live, base, sums, far_sums, ups):
    rows, half = base.shape
    return pl.pallas_call(
        final_kernel,
        in_specs=[SMEM, SMEM] + [VMEM] * 4,
        out_specs=VMEM,
        out_shape=jax.ShapeDtypeStruct((rows, half), jnp.bfloat16),
        compiler_params=kernel_params(12),
        cost_estimate=LIGHT,
    )(place, live, base, sums, far_sums, ups)


def per_device_planes(
    tokens,
    key_projection_weight,
    adapter_down_weight,
    adapter_up_weight,
    adapter_pool_index,
    block_adapter_index,
    block_live_tokens,
):
    place = jnp.stack(
        [lax.axis_index("groups"), lax.axis_index("dp"), lax.axis_index("tensor")]
    ).astype(jnp.int32)
    down, up = adapter_down_weight[0], adapter_up_weight[0]
    width, half = down.shape[1] // 2, up.shape[1] // 2
    piece = width + half
    own = jnp.concatenate([down, up], axis=1)
    first = lax.axis_index("groups") == 0
    own_ = lax.optimization_barrier(own)
    own_half = jnp.concatenate(
        [
            jnp.where(first, own_[:, :width], own_[:, width : 2 * width]),
            jnp.where(first, own_[:, 2 * width : 2 * width + half], own_[:, 2 * width + half :]),
        ],
        axis=1,
    )

    def ring(array, step):
        pairs = [(2 * z + y, 2 * ((z + step) % 4) + y) for z in range(4) for y in range(2)]
        return lax.ppermute(array, "dp", pairs)

    def over_y(array):
        return lax.ppermute(array, "dp", [(i, i ^ 1) for i in range(8)])

    def over_x(array):
        return lax.ppermute(array, "groups", SWAP)

    def over_cores(array):
        return lax.ppermute(array, "tensor", SWAP)

    scalars = (place, adapter_pool_index, block_adapter_index[:, 0])
    weight = key_projection_weight
    z1 = ring(own_half, 1)
    y0 = over_y(own)
    z3 = ring(own_half, -1)
    features = up.shape[1]
    *fars, mine_a = base_sums(
        place,
        tokens,
        weight,
        [(True, 0, features, FAR_PARTS), (False, 0, features // 2, 1)],
        LIGHT,
    )
    z1_ = after(z1, fars[0])
    x1 = over_x(z1_)
    y1 = over_y(z1_)
    z3_ = after(z3, z1_)
    z2a = ring(after(z1_, z3), 1)
    x3 = over_x(z3_)
    y3 = over_y(after(z3_, y0))
    z2b = ring(x1, 1)
    y2a = over_y(z2a)
    x1y = over_x(y1)

    (mine_b,) = base_sums(
        place,
        after(tokens, z3_, y0),
        weight,
        [(False, features // 2, features // 2, 1)],
        HEAVY,
    )
    def named(first, entries):
        return [
            (entry, kind, (first + at, 0), (first + at, width), half)
            for at, (entry, kind) in enumerate(entries)
        ]

    prior = shrink_sums(
        scalars,
        after(tokens, mine_b, x1, y1, z2a),
        [down, up, y0, z1, z3],
        [
            (0, "a", (0, 0), (1, 0), half),
            (0, "b", (0, width), (1, half), half),
            (1, "a", (2, 0), (2, 2 * width), half),
            (1, "b", (2, width), (2, 2 * width + half), half),
        ]
        + named(3, [(2, "own"), (6, "own")]),
        [],
        HEAVY,
    )
    x3y = over_x(y3)
    y2b = over_y(after(z2b, prior[0]))
    prior = shrink_sums(
        scalars,
        after(tokens, z2b),
        [x1, y1, z2a, x3, y3],
        named(0, [(2, "far"), (3, "own"), (4, "own"), (6, "far"), (7, "own")]),
        prior,
        LIGHT,
    )
    base_fars = [over_cores(after(far, prior[0])) for far in fars]
    prior = shrink_sums(
        scalars,
        tokens,
        [z2b, x1y, x3y, y2a],
        named(0, [(4, "far"), (3, "far"), (7, "far"), (5, "own")]),
        prior,
        HEAVY,
    )
    mine = jnp.concatenate([mine_a, mine_b], axis=1)
    base = mine + jnp.concatenate(base_fars, axis=0)
    sums, ups = shrink_sums(
        scalars, tokens, [y2b], named(0, [(5, "far")]), prior, LIGHT
    )
    far_sums = over_cores(sums)
    return final_keys(place, block_live_tokens, base, sums, far_sums, ups)


def per_device_gathered(
    tokens,
    key_projection_weight,
    adapter_down_weight,
    adapter_up_weight,
    adapter_pool_index,
    block_adapter_index,
    block_live_tokens,
):
    rows = tokens.shape[0]
    blocks = rows // BLK
    first_block = lax.axis_index("dp") * blocks
    slots = lax.dynamic_slice_in_dim(
        adapter_pool_index[block_adapter_index[:, 0]], first_block, blocks
    )
    fill = lax.dynamic_slice_in_dim(block_live_tokens, first_block, blocks)
    base_part = jnp.dot(tokens, key_projection_weight, preferred_element_type=jnp.float32)
    down = lax.all_gather(adapter_down_weight, "dp", axis=0, tiled=True)
    up = lax.all_gather(adapter_up_weight, "dp", axis=0, tiled=True)
    token_blocks = tokens.reshape(blocks, BLK, tokens.shape[1])
    shrink = jnp.einsum(
        "nrd,nbd->rnb",
        jnp.take(down, slots, axis=0),
        token_blocks,
        preferred_element_type=jnp.float32,
    )
    shrink = lax.psum(shrink.reshape(ADAPTER_RANK, rows), "tensor")
    delta = jnp.einsum(
        "rnb,nrc->nbc",
        shrink.reshape(ADAPTER_RANK, blocks, BLK),
        jnp.take(up, slots, axis=0).astype(jnp.float32),
        precision=lax.Precision.HIGHEST,
        preferred_element_type=jnp.float32,
    )
    base = lax.psum_scatter(base_part, "tensor", scatter_dimension=1, tiled=True)
    mask = jnp.arange(BLK, dtype=jnp.int32)[None, :] < fill[:, None]
    keys = base + delta.reshape(rows, base.shape[1])
    return jnp.where(mask.reshape(rows, 1), keys, 0.0).astype(jnp.bfloat16)


def solution(mesh):
    in_specs = (
        P(("groups", "dp"), "tensor"),
        P("tensor", None),
        P("dp", None, "tensor"),
        P("dp", None, "tensor"),
        P(),
        P("groups", None),
        P("groups"),
    )
    out_specs = P(("groups", "dp"), "tensor")
    planes = dict(mesh.shape) == {"groups": 2, "dp": 8, "tensor": 2}
    return jax.shard_map(
        per_device_planes if planes else per_device_gathered,
        mesh=mesh,
        in_specs=in_specs,
        out_specs=out_specs,
        check_vma=False,
    )
```

```python
import functools

import jax
import jax.numpy as jnp
from jax import lax
from jax.experimental import pallas as pl
from jax.experimental.pallas import tpu as pltpu
from jax.sharding import PartitionSpec as P

ADAPTER_RANK = 64
BLK = 128
FAR_PARTS = 3
SWAP = [(0, 1), (1, 0)]
NT = (((1,), (1,)), ((), ()))
TN = (((0,), (0,)), ((), ()))


def kernel_params(mebibytes):
    return pltpu.CompilerParams(vmem_limit_bytes=mebibytes * 1024 * 1024)


LIGHT = pl.CostEstimate(flops=1, bytes_accessed=1, transcendentals=0)
HEAVY = pl.CostEstimate(flops=30000000000, bytes_accessed=1, transcendentals=0)


def after(array, *others):
    return lax.optimization_barrier((array, *others))[0]


SMEM = pl.BlockSpec(memory_space=pltpu.SMEM)
VMEM = pl.BlockSpec(memory_space=pltpu.VMEM)
ANY = pl.BlockSpec(memory_space=pl.ANY)


def base_kernel(cuts, other, place, tokens, weight, *refs):
    core = 1 - place[2] if other else place[2]
    base_steps(cuts, core, tokens, weight, refs[:-4], refs[-4:])


def base_steps(cuts, core, tokens, weight, outs, scratch):
    tokens_v, weight_v, t_sem, w_sem = scratch
    part, half = outs[0].shape
    columns = pl.ds(pl.multiple_of(core * half, half), half)
    copies = []
    for step, (start, depth) in enumerate(cuts):
        span = pl.ds(start, depth)
        pair = (
            pltpu.make_async_copy(tokens.at[:, span], tokens_v.at[:, span], t_sem.at[step]),
            pltpu.make_async_copy(weight.at[span, columns], weight_v.at[span, :], w_sem.at[step]),
        )
        for copy in pair:
            copy.start()
        copies.append(pair)
    for step, (start, depth) in enumerate(cuts):
        for copy in copies[step]:
            copy.wait()
        for at, out in enumerate(outs):
            product = jnp.dot(
                tokens_v[pl.ds(at * part, part), pl.ds(start, depth)],
                weight_v[pl.ds(start, depth), :],
                preferred_element_type=jnp.float32,
            )
            out[...] = product if step == 0 else out[...] + product


def base_cuts(width):
    eighth = width // 8
    return [(0, eighth)] + [(at * eighth, 2 * eighth) for at in (1, 3, 5)] + [(7 * eighth, eighth)]


def base_scratch(tokens, weight):
    rows, width = tokens.shape
    steps = len(base_cuts(width))
    return [
        pltpu.VMEM((rows, width), tokens.dtype),
        pltpu.VMEM((width, weight.shape[1] // 2), weight.dtype),
        pltpu.SemaphoreType.DMA((steps,)),
        pltpu.SemaphoreType.DMA((steps,)),
    ]


def base_sums(place, tokens, weight, other, parts, hint):
    rows, width = tokens.shape
    half = weight.shape[1] // 2
    return pl.pallas_call(
        functools.partial(base_kernel, base_cuts(width), other),
        in_specs=[SMEM, ANY, ANY],
        out_specs=[VMEM] * parts,
        out_shape=[jax.ShapeDtypeStruct((rows // parts, half), jnp.float32)] * parts,
        scratch_shapes=base_scratch(tokens, weight),
        compiler_params=kernel_params(50),
        cost_estimate=hint,
    )(place, tokens, weight)


def entry_of(place, slot):
    back = ((place[1] >> 1) - (slot >> 1)) & 3
    return 2 * back + ((slot ^ place[1]) & 1)


def side_of(place, kind):
    return {"a": 0, "b": 1, "own": place[0], "far": 1 - place[0]}[kind]


def start_maps(pieces, entry_at, place, arrays, maps_v, up_map, sems, start_tokens):
    m_sem, u_sem = sems
    blocks, _, _, wide = maps_v.shape

    def start(block, carry):
        entry = entry_at(block)
        for at_entry, kind, (at, column), (up_at, up_column), half in pieces:

            @pl.when(entry == at_entry)
            def _(kind=kind, at=at, column=column, up_at=up_at, up_column=up_column):
                side = side_of(place, kind)
                start_tokens(block, side)
                pltpu.make_async_copy(
                    arrays[at].at[:, column : column + wide],
                    maps_v.at[block, side],
                    m_sem.at[block, side],
                ).start()
                pltpu.make_async_copy(
                    arrays[up_at].at[:, up_column : up_column + half],
                    up_map.at[block, :, pl.ds(pl.multiple_of(side * half, half), half)],
                    u_sem.at[block, side],
                ).start()

        return carry

    lax.fori_loop(0, blocks, start, 0)


def add_maps(pieces, entry_at, place, maps_v, tokens_v, up_map, sums, sems, wait_tokens):
    m_sem, u_sem = sems
    blocks, _, _, wide = maps_v.shape
    half = up_map.shape[2] // 2
    masks = []
    for side in range(2):
        bits = {"a": 0, "b": 0, "own": 0, "far": 0}
        for entry, kind, *_ in pieces:
            bits[kind] |= 1 << entry
        masks.append(
            bits["a" if side == 0 else "b"]
            | jnp.where(place[0] == side, bits["own"], bits["far"])
        )

    def add(block, carry):
        entry = entry_at(block)
        for side in range(2):

            @pl.when(((masks[side] >> entry) & 1) == 1)
            def _(side=side):
                wait_tokens(block, side)
                pltpu.make_async_copy(
                    maps_v.at[block, side], maps_v.at[block, side], m_sem.at[block, side]
                ).wait()
                sums[block] += lax.dot_general(
                    maps_v[block, side],
                    tokens_v[pl.ds(pl.multiple_of(block * BLK, BLK), BLK), pl.ds(side * wide, wide)],
                    NT,
                    preferred_element_type=jnp.float32,
                )
                half_map = up_map.at[block, :, pl.ds(side * half, half)]
                pltpu.make_async_copy(half_map, half_map, u_sem.at[block, side]).wait()

        return carry

    lax.fori_loop(0, blocks, add, 0)


def map_scratch(blocks, wide, dtype):
    return [
        pltpu.VMEM((blocks, 2, ADAPTER_RANK, wide), dtype),
        pltpu.SemaphoreType.DMA((blocks, 2)),
        pltpu.SemaphoreType.DMA((blocks, 2)),
    ]


def shrink_kernel(pieces, count, prior_count, place, pool_index, adapter_index, tokens, *refs):
    arrays, priors = refs[:count], refs[count : count + prior_count]
    sums, up_map, tokens_v, t_sem, maps_v, m_sem, u_sem = refs[count + prior_count :]
    blocks, wide = sums.shape[0], maps_v.shape[3]

    def entry_at(block):
        return entry_of(place, pool_index[adapter_index[place[1] * blocks + block]])

    def token_copy(block, side):
        place_of = (
            pl.ds(pl.multiple_of(block * BLK, BLK), BLK),
            pl.ds(pl.multiple_of(side * wide, wide), wide),
        )
        return pltpu.make_async_copy(
            tokens.at[place_of], tokens_v.at[place_of], t_sem.at[block, side]
        )

    start_maps(
        pieces, entry_at, place, arrays, maps_v, up_map, (m_sem, u_sem),
        lambda block, side: token_copy(block, side).start(),
    )
    sums[...] = priors[0][...] if priors else jnp.zeros_like(sums)
    add_maps(
        pieces, entry_at, place, maps_v, tokens_v, up_map, sums, (m_sem, u_sem),
        lambda block, side: token_copy(block, side).wait(),
    )


def shrink_sums(scalars, tokens, arrays, pieces, prior, hint):
    rows, width = tokens.shape
    blocks, count = rows // BLK, len(arrays)
    half = pieces[0][-1]
    return pl.pallas_call(
        functools.partial(shrink_kernel, pieces, count, len(prior)),
        in_specs=[SMEM, SMEM, SMEM] + [ANY] * (1 + count) + [VMEM, ANY][: len(prior)],
        out_specs=[VMEM, ANY],
        out_shape=[
            jax.ShapeDtypeStruct((blocks, ADAPTER_RANK, BLK), jnp.float32),
            jax.ShapeDtypeStruct((blocks, ADAPTER_RANK, 2 * half), jnp.bfloat16),
        ],
        input_output_aliases={5 + count: 1} if prior else {},
        scratch_shapes=[
            pltpu.VMEM((rows, width), tokens.dtype),
            pltpu.SemaphoreType.DMA((blocks, 2)),
        ]
        + map_scratch(blocks, width // 2, tokens.dtype),
        compiler_params=kernel_params(50),
        cost_estimate=hint,
    )(*scalars, tokens, *arrays, *prior)


def final_kernel(place, live, base, sums, far_sums, ups, keys):
    blocks, _, half = ups.shape
    for block in range(blocks):
        total = sums[block] + far_sums[block]
        high = total.astype(jnp.bfloat16)
        rest = total - high.astype(jnp.float32)
        middle = rest.astype(jnp.bfloat16)
        low = (rest - middle.astype(jnp.float32)).astype(jnp.bfloat16)
        up = ups[block]
        delta = lax.dot_general(
            jnp.concatenate([high, middle, low], axis=0),
            jnp.concatenate([up, up, up], axis=0),
            TN,
            preferred_element_type=jnp.float32,
        )
        row = lax.broadcasted_iota(jnp.int32, (BLK, half), 0)
        fill = live[place[1] * blocks + block]
        span = slice(block * BLK, (block + 1) * BLK)
        keys[span, :] = jnp.where(row < fill, base[span, :] + delta, 0.0).astype(keys.dtype)


def final_keys(place, live, base, sums, far_sums, ups):
    rows, half = base.shape
    return pl.pallas_call(
        final_kernel,
        in_specs=[SMEM, SMEM] + [VMEM] * 4,
        out_specs=VMEM,
        out_shape=jax.ShapeDtypeStruct((rows, half), jnp.bfloat16),
        compiler_params=kernel_params(12),
        cost_estimate=LIGHT,
    )(place, live, base, sums, far_sums, ups)


def per_device_planes(
    tokens,
    key_projection_weight,
    adapter_down_weight,
    adapter_up_weight,
    adapter_pool_index,
    block_adapter_index,
    block_live_tokens,
):
    place = jnp.stack(
        [lax.axis_index("groups"), lax.axis_index("dp"), lax.axis_index("tensor")]
    ).astype(jnp.int32)
    down, up = adapter_down_weight[0], adapter_up_weight[0]
    width, half = down.shape[1] // 2, up.shape[1] // 2
    piece = width + half
    own = jnp.concatenate([down, up], axis=1)
    first = lax.axis_index("groups") == 0
    own_ = lax.optimization_barrier(own)
    own_half = jnp.concatenate(
        [
            jnp.where(first, own_[:, :width], own_[:, width : 2 * width]),
            jnp.where(first, own_[:, 2 * width : 2 * width + half], own_[:, 2 * width + half :]),
        ],
        axis=1,
    )

    def ring(array, step):
        pairs = [(2 * z + y, 2 * ((z + step) % 4) + y) for z in range(4) for y in range(2)]
        return lax.ppermute(array, "dp", pairs)

    def over_y(array):
        return lax.ppermute(array, "dp", [(i, i ^ 1) for i in range(8)])

    def over_x(array):
        return lax.ppermute(array, "groups", SWAP)

    def over_cores(array):
        return lax.ppermute(array, "tensor", SWAP)

    scalars = (place, adapter_pool_index, block_adapter_index[:, 0])
    weight = key_projection_weight
    z1 = ring(own_half, 1)
    y0 = over_y(own)
    z3 = ring(own_half, -1)
    fars = base_sums(place, tokens, weight, True, FAR_PARTS, LIGHT)
    z1_ = after(z1, fars[0])
    x1 = over_x(z1_)
    y1 = over_y(z1_)
    z3_ = after(z3, z1_)
    z2a = ring(after(z1_, z3), 1)
    x3 = over_x(z3_)
    y3 = over_y(after(z3_, y0))
    z2b = ring(x1, 1)
    y2a = over_y(after(z2a, y3))
    x1y = over_x(y1)

    (mine,) = base_sums(place, after(tokens, z3_, y0), weight, False, 1, HEAVY)
    def named(first, entries):
        return [
            (entry, kind, (first + at, 0), (first + at, width), half)
            for at, (entry, kind) in enumerate(entries)
        ]

    prior = shrink_sums(
        scalars,
        after(tokens, mine, x1, y1, z2a, y3),
        [down, up, y0, z1, z3],
        [
            (0, "a", (0, 0), (1, 0), half),
            (0, "b", (0, width), (1, half), half),
            (1, "a", (2, 0), (2, 2 * width), half),
            (1, "b", (2, width), (2, 2 * width + half), half),
        ]
        + named(3, [(2, "own"), (6, "own")]),
        [],
        HEAVY,
    )
    x3y = over_x(y3)
    y2b = over_y(after(z2b, prior[0]))
    prior = shrink_sums(
        scalars,
        after(tokens, z2b),
        [x1, y1, z2a, x3, y3],
        named(0, [(2, "far"), (3, "own"), (4, "own"), (6, "far"), (7, "own")]),
        prior,
        LIGHT,
    )
    base_fars = [over_cores(after(far, prior[0])) for far in fars]
    prior = shrink_sums(
        scalars,
        tokens,
        [z2b, x1y, x3y, y2a],
        named(0, [(4, "far"), (3, "far"), (7, "far"), (5, "own")]),
        prior,
        HEAVY,
    )
    base = mine + jnp.concatenate(base_fars, axis=0)
    sums, ups = shrink_sums(
        scalars, tokens, [y2b], named(0, [(5, "far")]), prior, LIGHT
    )
    far_sums = over_cores(sums)
    return final_keys(place, block_live_tokens, base, sums, far_sums, ups)


def per_device_gathered(
    tokens,
    key_projection_weight,
    adapter_down_weight,
    adapter_up_weight,
    adapter_pool_index,
    block_adapter_index,
    block_live_tokens,
):
    rows = tokens.shape[0]
    blocks = rows // BLK
    first_block = lax.axis_index("dp") * blocks
    slots = lax.dynamic_slice_in_dim(
        adapter_pool_index[block_adapter_index[:, 0]], first_block, blocks
    )
    fill = lax.dynamic_slice_in_dim(block_live_tokens, first_block, blocks)
    base_part = jnp.dot(tokens, key_projection_weight, preferred_element_type=jnp.float32)
    down = lax.all_gather(adapter_down_weight, "dp", axis=0, tiled=True)
    up = lax.all_gather(adapter_up_weight, "dp", axis=0, tiled=True)
    token_blocks = tokens.reshape(blocks, BLK, tokens.shape[1])
    shrink = jnp.einsum(
        "nrd,nbd->rnb",
        jnp.take(down, slots, axis=0),
        token_blocks,
        preferred_element_type=jnp.float32,
    )
    shrink = lax.psum(shrink.reshape(ADAPTER_RANK, rows), "tensor")
    delta = jnp.einsum(
        "rnb,nrc->nbc",
        shrink.reshape(ADAPTER_RANK, blocks, BLK),
        jnp.take(up, slots, axis=0).astype(jnp.float32),
        precision=lax.Precision.HIGHEST,
        preferred_element_type=jnp.float32,
    )
    base = lax.psum_scatter(base_part, "tensor", scatter_dimension=1, tiled=True)
    mask = jnp.arange(BLK, dtype=jnp.int32)[None, :] < fill[:, None]
    keys = base + delta.reshape(rows, base.shape[1])
    return jnp.where(mask.reshape(rows, 1), keys, 0.0).astype(jnp.bfloat16)


def solution(mesh):
    in_specs = (
        P(("groups", "dp"), "tensor"),
        P("tensor", None),
        P("dp", None, "tensor"),
        P("dp", None, "tensor"),
        P(),
        P("groups", None),
        P("groups"),
    )
    out_specs = P(("groups", "dp"), "tensor")
    planes = dict(mesh.shape) == {"groups": 2, "dp": 8, "tensor": 2}
    return jax.shard_map(
        per_device_planes if planes else per_device_gathered,
        mesh=mesh,
        in_specs=in_specs,
        out_specs=out_specs,
        check_vma=False,
    )
```

```python
import functools

import jax
import jax.numpy as jnp
from jax import lax
from jax.experimental import pallas as pl
from jax.experimental.pallas import tpu as pltpu
from jax.sharding import PartitionSpec as P

ADAPTER_RANK = 64
BLK = 128
FAR_PARTS = 3
SWAP = [(0, 1), (1, 0)]
NT = (((1,), (1,)), ((), ()))
TN = (((0,), (0,)), ((), ()))


def kernel_params(mebibytes):
    return pltpu.CompilerParams(vmem_limit_bytes=mebibytes * 1024 * 1024)


LIGHT = pl.CostEstimate(flops=1, bytes_accessed=1, transcendentals=0)
HEAVY = pl.CostEstimate(flops=30000000000, bytes_accessed=1, transcendentals=0)


def after(array, *others):
    return lax.optimization_barrier((array, *others))[0]


SMEM = pl.BlockSpec(memory_space=pltpu.SMEM)
VMEM = pl.BlockSpec(memory_space=pltpu.VMEM)
ANY = pl.BlockSpec(memory_space=pl.ANY)


def base_kernel(cuts, other, place, tokens, weight, *refs):
    core = 1 - place[2] if other else place[2]
    base_steps(cuts, core, tokens, weight, refs[:-4], refs[-4:])


def base_steps(cuts, core, tokens, weight, outs, scratch):
    tokens_v, weight_v, t_sem, w_sem = scratch
    part, half = outs[0].shape
    columns = pl.ds(pl.multiple_of(core * half, half), half)
    copies = []
    for step, (start, depth) in enumerate(cuts):
        span = pl.ds(start, depth)
        pair = (
            pltpu.make_async_copy(tokens.at[:, span], tokens_v.at[:, span], t_sem.at[step]),
            pltpu.make_async_copy(weight.at[span, columns], weight_v.at[span, :], w_sem.at[step]),
        )
        for copy in pair:
            copy.start()
        copies.append(pair)
    for step, (start, depth) in enumerate(cuts):
        for copy in copies[step]:
            copy.wait()
        for at, out in enumerate(outs):
            product = jnp.dot(
                tokens_v[pl.ds(at * part, part), pl.ds(start, depth)],
                weight_v[pl.ds(start, depth), :],
                preferred_element_type=jnp.float32,
            )
            out[...] = product if step == 0 else out[...] + product


def base_cuts(width):
    eighth = width // 8
    return [(0, eighth)] + [(at * eighth, 2 * eighth) for at in (1, 3, 5)] + [(7 * eighth, eighth)]


def base_scratch(tokens, weight):
    rows, width = tokens.shape
    steps = len(base_cuts(width))
    return [
        pltpu.VMEM((rows, width), tokens.dtype),
        pltpu.VMEM((width, weight.shape[1] // 2), weight.dtype),
        pltpu.SemaphoreType.DMA((steps,)),
        pltpu.SemaphoreType.DMA((steps,)),
    ]


def base_sums(place, tokens, weight, other, parts, hint):
    rows, width = tokens.shape
    half = weight.shape[1] // 2
    return pl.pallas_call(
        functools.partial(base_kernel, base_cuts(width), other),
        in_specs=[SMEM, ANY, ANY],
        out_specs=[VMEM] * parts,
        out_shape=[jax.ShapeDtypeStruct((rows // parts, half), jnp.float32)] * parts,
        scratch_shapes=base_scratch(tokens, weight),
        compiler_params=kernel_params(50),
        cost_estimate=hint,
    )(place, tokens, weight)


def entry_of(place, slot):
    back = ((place[1] >> 1) - (slot >> 1)) & 3
    return 2 * back + ((slot ^ place[1]) & 1)


def side_of(place, kind):
    return {"a": 0, "b": 1, "own": place[0], "far": 1 - place[0]}[kind]


def start_maps(pieces, entry_at, place, arrays, maps_v, up_map, sems, start_tokens):
    m_sem, u_sem = sems
    blocks, _, _, wide = maps_v.shape

    def start(block, carry):
        entry = entry_at(block)
        for at_entry, kind, (at, column), (up_at, up_column), half in pieces:

            @pl.when(entry == at_entry)
            def _(kind=kind, at=at, column=column, up_at=up_at, up_column=up_column):
                side = side_of(place, kind)
                start_tokens(block, side)
                pltpu.make_async_copy(
                    arrays[at].at[:, column : column + wide],
                    maps_v.at[block, side],
                    m_sem.at[block, side],
                ).start()
                pltpu.make_async_copy(
                    arrays[up_at].at[:, up_column : up_column + half],
                    up_map.at[block, :, pl.ds(pl.multiple_of(side * half, half), half)],
                    u_sem.at[block, side],
                ).start()

        return carry

    lax.fori_loop(0, blocks, start, 0)


def add_maps(pieces, entry_at, place, maps_v, tokens_v, up_map, sums, sems, wait_tokens):
    m_sem, u_sem = sems
    blocks, _, _, wide = maps_v.shape
    half = up_map.shape[2] // 2
    masks = []
    for side in range(2):
        bits = {"a": 0, "b": 0, "own": 0, "far": 0}
        for entry, kind, *_ in pieces:
            bits[kind] |= 1 << entry
        masks.append(
            bits["a" if side == 0 else "b"]
            | jnp.where(place[0] == side, bits["own"], bits["far"])
        )

    def add(block, carry):
        entry = entry_at(block)
        for side in range(2):

            @pl.when(((masks[side] >> entry) & 1) == 1)
            def _(side=side):
                wait_tokens(block, side)
                pltpu.make_async_copy(
                    maps_v.at[block, side], maps_v.at[block, side], m_sem.at[block, side]
                ).wait()
                sums[block] += lax.dot_general(
                    maps_v[block, side],
                    tokens_v[pl.ds(pl.multiple_of(block * BLK, BLK), BLK), pl.ds(side * wide, wide)],
                    NT,
                    preferred_element_type=jnp.float32,
                )
                half_map = up_map.at[block, :, pl.ds(side * half, half)]
                pltpu.make_async_copy(half_map, half_map, u_sem.at[block, side]).wait()

        return carry

    lax.fori_loop(0, blocks, add, 0)


def map_scratch(blocks, wide, dtype):
    return [
        pltpu.VMEM((blocks, 2, ADAPTER_RANK, wide), dtype),
        pltpu.SemaphoreType.DMA((blocks, 2)),
        pltpu.SemaphoreType.DMA((blocks, 2)),
    ]


def shrink_kernel(pieces, count, prior_count, place, pool_index, adapter_index, tokens, *refs):
    arrays, priors = refs[:count], refs[count : count + prior_count]
    sums, up_map, tokens_v, t_sem, maps_v, m_sem, u_sem = refs[count + prior_count :]
    blocks, wide = sums.shape[0], maps_v.shape[3]

    def entry_at(block):
        return entry_of(place, pool_index[adapter_index[place[1] * blocks + block]])

    def token_copy(block, side):
        place_of = (
            pl.ds(pl.multiple_of(block * BLK, BLK), BLK),
            pl.ds(pl.multiple_of(side * wide, wide), wide),
        )
        return pltpu.make_async_copy(
            tokens.at[place_of], tokens_v.at[place_of], t_sem.at[block, side]
        )

    start_maps(
        pieces, entry_at, place, arrays, maps_v, up_map, (m_sem, u_sem),
        lambda block, side: token_copy(block, side).start(),
    )
    sums[...] = priors[0][...] if priors else jnp.zeros_like(sums)
    add_maps(
        pieces, entry_at, place, maps_v, tokens_v, up_map, sums, (m_sem, u_sem),
        lambda block, side: token_copy(block, side).wait(),
    )


def shrink_sums(scalars, tokens, arrays, pieces, prior, hint):
    rows, width = tokens.shape
    blocks, count = rows // BLK, len(arrays)
    half = pieces[0][-1]
    return pl.pallas_call(
        functools.partial(shrink_kernel, pieces, count, len(prior)),
        in_specs=[SMEM, SMEM, SMEM] + [ANY] * (1 + count) + [VMEM, ANY][: len(prior)],
        out_specs=[VMEM, ANY],
        out_shape=[
            jax.ShapeDtypeStruct((blocks, ADAPTER_RANK, BLK), jnp.float32),
            jax.ShapeDtypeStruct((blocks, ADAPTER_RANK, 2 * half), jnp.bfloat16),
        ],
        input_output_aliases={5 + count: 1} if prior else {},
        scratch_shapes=[
            pltpu.VMEM((rows, width), tokens.dtype),
            pltpu.SemaphoreType.DMA((blocks, 2)),
        ]
        + map_scratch(blocks, width // 2, tokens.dtype),
        compiler_params=kernel_params(50),
        cost_estimate=hint,
    )(*scalars, tokens, *arrays, *prior)


def final_kernel(place, live, base, sums, far_sums, ups, keys):
    blocks, _, half = ups.shape
    for block in range(blocks):
        total = sums[block] + far_sums[block]
        high = total.astype(jnp.bfloat16)
        rest = total - high.astype(jnp.float32)
        middle = rest.astype(jnp.bfloat16)
        low = (rest - middle.astype(jnp.float32)).astype(jnp.bfloat16)
        up = ups[block]
        delta = lax.dot_general(
            jnp.concatenate([high, middle, low], axis=0),
            jnp.concatenate([up, up, up], axis=0),
            TN,
            preferred_element_type=jnp.float32,
        )
        row = lax.broadcasted_iota(jnp.int32, (BLK, half), 0)
        fill = live[place[1] * blocks + block]
        span = slice(block * BLK, (block + 1) * BLK)
        keys[span, :] = jnp.where(row < fill, base[span, :] + delta, 0.0).astype(keys.dtype)


def final_keys(place, live, base, sums, far_sums, ups):
    rows, half = base.shape
    return pl.pallas_call(
        final_kernel,
        in_specs=[SMEM, SMEM] + [VMEM] * 4,
        out_specs=VMEM,
        out_shape=jax.ShapeDtypeStruct((rows, half), jnp.bfloat16),
        compiler_params=kernel_params(12),
        cost_estimate=LIGHT,
    )(place, live, base, sums, far_sums, ups)


def per_device_planes(
    tokens,
    key_projection_weight,
    adapter_down_weight,
    adapter_up_weight,
    adapter_pool_index,
    block_adapter_index,
    block_live_tokens,
):
    place = jnp.stack(
        [lax.axis_index("groups"), lax.axis_index("dp"), lax.axis_index("tensor")]
    ).astype(jnp.int32)
    down, up = adapter_down_weight[0], adapter_up_weight[0]
    width, half = down.shape[1] // 2, up.shape[1] // 2
    piece = width + half
    own = jnp.concatenate([down, up], axis=1)
    first = lax.axis_index("groups") == 0
    own_ = lax.optimization_barrier(own)
    own_half = jnp.concatenate(
        [
            jnp.where(first, own_[:, :width], own_[:, width : 2 * width]),
            jnp.where(first, own_[:, 2 * width : 2 * width + half], own_[:, 2 * width + half :]),
        ],
        axis=1,
    )

    def ring(array, step):
        pairs = [(2 * z + y, 2 * ((z + step) % 4) + y) for z in range(4) for y in range(2)]
        return lax.ppermute(array, "dp", pairs)

    def over_y(array):
        return lax.ppermute(array, "dp", [(i, i ^ 1) for i in range(8)])

    def over_x(array):
        return lax.ppermute(array, "groups", SWAP)

    def over_cores(array):
        return lax.ppermute(array, "tensor", SWAP)

    scalars = (place, adapter_pool_index, block_adapter_index[:, 0])
    weight = key_projection_weight
    z1 = ring(own_half, 1)
    y0 = over_y(own)
    z3 = ring(own_half, -1)
    fars = base_sums(place, tokens, weight, True, FAR_PARTS, LIGHT)
    z1_ = after(z1, fars[0])
    x1 = over_x(z1_)
    y1 = over_y(z1_)

    def named(first, entries):
        return [
            (entry, kind, (first + at, 0), (first + at, width), half)
            for at, (entry, kind) in enumerate(entries)
        ]

    prior = shrink_sums(
        scalars,
        after(tokens, z1_, y0),
        [down, up, y0, z1],
        [
            (0, "a", (0, 0), (1, 0), half),
            (0, "b", (0, width), (1, half), half),
            (1, "a", (2, 0), (2, 2 * width), half),
            (1, "b", (2, width), (2, 2 * width + half), half),
        ]
        + named(3, [(2, "own")]),
        [],
        HEAVY,
    )
    z3_ = after(z3, prior[0])
    z2a = ring(after(z1_, z3_), 1)
    x3 = over_x(z3_)
    y3 = over_y(after(z3_, y0))
    z2b = ring(x1, 1)
    y2a = over_y(after(z2a, y3))
    x1y = over_x(y1)
    (mine,) = base_sums(place, after(tokens, z3_, y0), weight, False, 1, HEAVY)
    prior = shrink_sums(
        scalars,
        after(tokens, mine, x1, y1, z2a, y3),
        [z3, x1, y1, z2a, y3],
        named(0, [(6, "own"), (2, "far"), (3, "own"), (4, "own"), (7, "own")]),
        prior,
        HEAVY,
    )
    x3y = over_x(y3)
    y2b = over_y(after(z2b, prior[0]))
    prior = shrink_sums(
        scalars, tokens, [x3, z2b], named(0, [(6, "far"), (4, "far")]), prior, LIGHT
    )
    base_fars = [over_cores(after(far, prior[0])) for far in fars]
    prior = shrink_sums(
        scalars,
        tokens,
        [x1y, x3y, y2a],
        named(0, [(3, "far"), (7, "far"), (5, "own")]),
        prior,
        HEAVY,
    )
    base = mine + jnp.concatenate(base_fars, axis=0)
    sums, ups = shrink_sums(
        scalars, tokens, [y2b], named(0, [(5, "far")]), prior, LIGHT
    )
    far_sums = over_cores(sums)
    return final_keys(place, block_live_tokens, base, sums, far_sums, ups)


def per_device_gathered(
    tokens,
    key_projection_weight,
    adapter_down_weight,
    adapter_up_weight,
    adapter_pool_index,
    block_adapter_index,
    block_live_tokens,
):
    rows = tokens.shape[0]
    blocks = rows // BLK
    first_block = lax.axis_index("dp") * blocks
    slots = lax.dynamic_slice_in_dim(
        adapter_pool_index[block_adapter_index[:, 0]], first_block, blocks
    )
    fill = lax.dynamic_slice_in_dim(block_live_tokens, first_block, blocks)
    base_part = jnp.dot(tokens, key_projection_weight, preferred_element_type=jnp.float32)
    down = lax.all_gather(adapter_down_weight, "dp", axis=0, tiled=True)
    up = lax.all_gather(adapter_up_weight, "dp", axis=0, tiled=True)
    token_blocks = tokens.reshape(blocks, BLK, tokens.shape[1])
    shrink = jnp.einsum(
        "nrd,nbd->rnb",
        jnp.take(down, slots, axis=0),
        token_blocks,
        preferred_element_type=jnp.float32,
    )
    shrink = lax.psum(shrink.reshape(ADAPTER_RANK, rows), "tensor")
    delta = jnp.einsum(
        "rnb,nrc->nbc",
        shrink.reshape(ADAPTER_RANK, blocks, BLK),
        jnp.take(up, slots, axis=0).astype(jnp.float32),
        precision=lax.Precision.HIGHEST,
        preferred_element_type=jnp.float32,
    )
    base = lax.psum_scatter(base_part, "tensor", scatter_dimension=1, tiled=True)
    mask = jnp.arange(BLK, dtype=jnp.int32)[None, :] < fill[:, None]
    keys = base + delta.reshape(rows, base.shape[1])
    return jnp.where(mask.reshape(rows, 1), keys, 0.0).astype(jnp.bfloat16)


def solution(mesh):
    in_specs = (
        P(("groups", "dp"), "tensor"),
        P("tensor", None),
        P("dp", None, "tensor"),
        P("dp", None, "tensor"),
        P(),
        P("groups", None),
        P("groups"),
    )
    out_specs = P(("groups", "dp"), "tensor")
    planes = dict(mesh.shape) == {"groups": 2, "dp": 8, "tensor": 2}
    return jax.shard_map(
        per_device_planes if planes else per_device_gathered,
        mesh=mesh,
        in_specs=in_specs,
        out_specs=out_specs,
        check_vma=False,
    )
```

```python
import functools

import jax
import jax.numpy as jnp
from jax import lax
from jax.experimental import pallas as pl
from jax.experimental.pallas import tpu as pltpu
from jax.sharding import PartitionSpec as P

ADAPTER_RANK = 64
BLK = 128
FAR_PARTS = 3
SWAP = [(0, 1), (1, 0)]
NT = (((1,), (1,)), ((), ()))
TN = (((0,), (0,)), ((), ()))


def kernel_params(mebibytes):
    return pltpu.CompilerParams(vmem_limit_bytes=mebibytes * 1024 * 1024)


LIGHT = pl.CostEstimate(flops=1, bytes_accessed=1, transcendentals=0)
HEAVY = pl.CostEstimate(flops=30000000000, bytes_accessed=1, transcendentals=0)


def after(array, *others):
    return lax.optimization_barrier((array, *others))[0]


SMEM = pl.BlockSpec(memory_space=pltpu.SMEM)
VMEM = pl.BlockSpec(memory_space=pltpu.VMEM)
ANY = pl.BlockSpec(memory_space=pl.ANY)


def base_kernel(cuts, other, place, tokens, weight, *refs):
    core = 1 - place[2] if other else place[2]
    base_steps(cuts, core, tokens, weight, refs[:-4], refs[-4:])


def base_steps(cuts, core, tokens, weight, outs, scratch):
    tokens_v, weight_v, t_sem, w_sem = scratch
    part, half = outs[0].shape
    columns = pl.ds(pl.multiple_of(core * half, half), half)
    copies = []
    for step, (start, depth) in enumerate(cuts):
        span = pl.ds(start, depth)
        pair = (
            pltpu.make_async_copy(tokens.at[:, span], tokens_v.at[:, span], t_sem.at[step]),
            pltpu.make_async_copy(weight.at[span, columns], weight_v.at[span, :], w_sem.at[step]),
        )
        for copy in pair:
            copy.start()
        copies.append(pair)
    for step, (start, depth) in enumerate(cuts):
        for copy in copies[step]:
            copy.wait()
        for at, out in enumerate(outs):
            product = jnp.dot(
                tokens_v[pl.ds(at * part, part), pl.ds(start, depth)],
                weight_v[pl.ds(start, depth), :],
                preferred_element_type=jnp.float32,
            )
            out[...] = product if step == 0 else out[...] + product


def base_cuts(width):
    eighth = width // 8
    return [(0, eighth)] + [(at * eighth, 2 * eighth) for at in (1, 3, 5)] + [(7 * eighth, eighth)]


def base_scratch(tokens, weight):
    rows, width = tokens.shape
    steps = len(base_cuts(width))
    return [
        pltpu.VMEM((rows, width), tokens.dtype),
        pltpu.VMEM((width, weight.shape[1] // 2), weight.dtype),
        pltpu.SemaphoreType.DMA((steps,)),
        pltpu.SemaphoreType.DMA((steps,)),
    ]


def base_sums(place, tokens, weight, other, parts, hint):
    rows, width = tokens.shape
    half = weight.shape[1] // 2
    return pl.pallas_call(
        functools.partial(base_kernel, base_cuts(width), other),
        in_specs=[SMEM, ANY, ANY],
        out_specs=[VMEM] * parts,
        out_shape=[jax.ShapeDtypeStruct((rows // parts, half), jnp.float32)] * parts,
        scratch_shapes=base_scratch(tokens, weight),
        compiler_params=kernel_params(50),
        cost_estimate=hint,
    )(place, tokens, weight)


def entry_of(place, slot):
    back = ((place[1] >> 1) - (slot >> 1)) & 3
    return 2 * back + ((slot ^ place[1]) & 1)


def side_of(place, kind):
    return {"a": 0, "b": 1, "own": place[0], "far": 1 - place[0]}[kind]


def start_maps(pieces, entry_at, place, arrays, maps_v, up_map, sems, start_tokens):
    m_sem, u_sem = sems
    blocks, _, _, wide = maps_v.shape

    def start(block, carry):
        entry = entry_at(block)
        for at_entry, kind, (at, column), (up_at, up_column), half in pieces:

            @pl.when(entry == at_entry)
            def _(kind=kind, at=at, column=column, up_at=up_at, up_column=up_column):
                side = side_of(place, kind)
                start_tokens(block, side)
                pltpu.make_async_copy(
                    arrays[at].at[:, column : column + wide],
                    maps_v.at[block, side],
                    m_sem.at[block, side],
                ).start()
                pltpu.make_async_copy(
                    arrays[up_at].at[:, up_column : up_column + half],
                    up_map.at[block, :, pl.ds(pl.multiple_of(side * half, half), half)],
                    u_sem.at[block, side],
                ).start()

        return carry

    lax.fori_loop(0, blocks, start, 0)


def add_maps(pieces, entry_at, place, maps_v, tokens_v, up_map, sums, sems, wait_tokens):
    m_sem, u_sem = sems
    blocks, _, _, wide = maps_v.shape
    half = up_map.shape[2] // 2
    masks = []
    for side in range(2):
        bits = {"a": 0, "b": 0, "own": 0, "far": 0}
        for entry, kind, *_ in pieces:
            bits[kind] |= 1 << entry
        masks.append(
            bits["a" if side == 0 else "b"]
            | jnp.where(place[0] == side, bits["own"], bits["far"])
        )

    def add(block, carry):
        entry = entry_at(block)
        for side in range(2):

            @pl.when(((masks[side] >> entry) & 1) == 1)
            def _(side=side):
                wait_tokens(block, side)
                pltpu.make_async_copy(
                    maps_v.at[block, side], maps_v.at[block, side], m_sem.at[block, side]
                ).wait()
                sums[block] += lax.dot_general(
                    maps_v[block, side],
                    tokens_v[pl.ds(pl.multiple_of(block * BLK, BLK), BLK), pl.ds(side * wide, wide)],
                    NT,
                    preferred_element_type=jnp.float32,
                )
                half_map = up_map.at[block, :, pl.ds(side * half, half)]
                pltpu.make_async_copy(half_map, half_map, u_sem.at[block, side]).wait()

        return carry

    lax.fori_loop(0, blocks, add, 0)


def map_scratch(blocks, wide, dtype):
    return [
        pltpu.VMEM((blocks, 2, ADAPTER_RANK, wide), dtype),
        pltpu.SemaphoreType.DMA((blocks, 2)),
        pltpu.SemaphoreType.DMA((blocks, 2)),
    ]


def shrink_kernel(pieces, count, prior_count, place, pool_index, adapter_index, tokens, *refs):
    arrays, priors = refs[:count], refs[count : count + prior_count]
    sums, up_map, tokens_v, t_sem, maps_v, m_sem, u_sem = refs[count + prior_count :]
    blocks, wide = sums.shape[0], maps_v.shape[3]

    def entry_at(block):
        return entry_of(place, pool_index[adapter_index[place[1] * blocks + block]])

    def token_copy(block, side):
        place_of = (
            pl.ds(pl.multiple_of(block * BLK, BLK), BLK),
            pl.ds(pl.multiple_of(side * wide, wide), wide),
        )
        return pltpu.make_async_copy(
            tokens.at[place_of], tokens_v.at[place_of], t_sem.at[block, side]
        )

    start_maps(
        pieces, entry_at, place, arrays, maps_v, up_map, (m_sem, u_sem),
        lambda block, side: token_copy(block, side).start(),
    )
    sums[...] = priors[0][...] if priors else jnp.zeros_like(sums)
    add_maps(
        pieces, entry_at, place, maps_v, tokens_v, up_map, sums, (m_sem, u_sem),
        lambda block, side: token_copy(block, side).wait(),
    )


def shrink_sums(scalars, tokens, arrays, pieces, prior, hint):
    rows, width = tokens.shape
    blocks, count = rows // BLK, len(arrays)
    half = pieces[0][-1]
    return pl.pallas_call(
        functools.partial(shrink_kernel, pieces, count, len(prior)),
        in_specs=[SMEM, SMEM, SMEM] + [ANY] * (1 + count) + [VMEM, ANY][: len(prior)],
        out_specs=[VMEM, ANY],
        out_shape=[
            jax.ShapeDtypeStruct((blocks, ADAPTER_RANK, BLK), jnp.float32),
            jax.ShapeDtypeStruct((blocks, ADAPTER_RANK, 2 * half), jnp.bfloat16),
        ],
        input_output_aliases={5 + count: 1} if prior else {},
        scratch_shapes=[
            pltpu.VMEM((rows, width), tokens.dtype),
            pltpu.SemaphoreType.DMA((blocks, 2)),
        ]
        + map_scratch(blocks, width // 2, tokens.dtype),
        compiler_params=kernel_params(50),
        cost_estimate=hint,
    )(*scalars, tokens, *arrays, *prior)


def final_kernel(place, live, base, sums, far_sums, ups, keys):
    blocks, _, half = ups.shape
    for block in range(blocks):
        total = sums[block] + far_sums[block]
        high = total.astype(jnp.bfloat16)
        rest = total - high.astype(jnp.float32)
        middle = rest.astype(jnp.bfloat16)
        low = (rest - middle.astype(jnp.float32)).astype(jnp.bfloat16)
        up = ups[block]
        delta = lax.dot_general(
            jnp.concatenate([high, middle, low], axis=0),
            jnp.concatenate([up, up, up], axis=0),
            TN,
            preferred_element_type=jnp.float32,
        )
        row = lax.broadcasted_iota(jnp.int32, (BLK, half), 0)
        fill = live[place[1] * blocks + block]
        span = slice(block * BLK, (block + 1) * BLK)
        keys[span, :] = jnp.where(row < fill, base[span, :] + delta, 0.0).astype(keys.dtype)


def final_keys(place, live, base, sums, far_sums, ups):
    rows, half = base.shape
    return pl.pallas_call(
        final_kernel,
        in_specs=[SMEM, SMEM] + [VMEM] * 4,
        out_specs=VMEM,
        out_shape=jax.ShapeDtypeStruct((rows, half), jnp.bfloat16),
        compiler_params=kernel_params(12),
        cost_estimate=LIGHT,
    )(place, live, base, sums, far_sums, ups)


def per_device_planes(
    tokens,
    key_projection_weight,
    adapter_down_weight,
    adapter_up_weight,
    adapter_pool_index,
    block_adapter_index,
    block_live_tokens,
):
    place = jnp.stack(
        [lax.axis_index("groups"), lax.axis_index("dp"), lax.axis_index("tensor")]
    ).astype(jnp.int32)
    down, up = adapter_down_weight[0], adapter_up_weight[0]
    width, half = down.shape[1] // 2, up.shape[1] // 2
    piece = width + half
    own = jnp.concatenate([down, up], axis=1)
    first = lax.axis_index("groups") == 0
    own_ = lax.optimization_barrier(own)
    own_half = jnp.concatenate(
        [
            jnp.where(first, own_[:, :width], own_[:, width : 2 * width]),
            jnp.where(first, own_[:, 2 * width : 2 * width + half], own_[:, 2 * width + half :]),
        ],
        axis=1,
    )

    def ring(array, step):
        pairs = [(2 * z + y, 2 * ((z + step) % 4) + y) for z in range(4) for y in range(2)]
        return lax.ppermute(array, "dp", pairs)

    def over_y(array):
        return lax.ppermute(array, "dp", [(i, i ^ 1) for i in range(8)])

    def over_x(array):
        return lax.ppermute(array, "groups", SWAP)

    def over_cores(array):
        return lax.ppermute(array, "tensor", SWAP)

    scalars = (place, adapter_pool_index, block_adapter_index[:, 0])
    weight = key_projection_weight
    z1 = ring(own_half, 1)
    y0 = over_y(own)
    z3 = ring(own_half, -1)
    fars = base_sums(place, tokens, weight, True, FAR_PARTS, LIGHT)
    z1_ = after(z1, fars[0])
    x1 = over_x(z1_)
    y1 = over_y(z1_)

    def named(first, entries):
        return [
            (entry, kind, (first + at, 0), (first + at, width), half)
            for at, (entry, kind) in enumerate(entries)
        ]

    prior = shrink_sums(
        scalars,
        after(tokens, z1_),
        [down, up],
        [(0, "a", (0, 0), (1, 0), half), (0, "b", (0, width), (1, half), half)],
        [],
        LIGHT,
    )
    z3_ = after(z3, z1_, prior[0])
    z2a = ring(after(z1_, z3_), 1)
    x3 = over_x(z3_)
    y3 = over_y(after(z3_, y0))
    z2b = ring(x1, 1)
    y2a = over_y(after(z2a, y3))
    x1y = over_x(y1)

    (mine,) = base_sums(place, after(tokens, z3_, y0), weight, False, 1, HEAVY)
    prior = shrink_sums(
        scalars,
        after(tokens, mine, x1, y1, z2a, y3),
        [y0, z1, z3],
        [
            (1, "a", (0, 0), (0, 2 * width), half),
            (1, "b", (0, width), (0, 2 * width + half), half),
        ]
        + named(1, [(2, "own"), (6, "own")]),
        prior,
        HEAVY,
    )
    x3y = over_x(y3)
    y2b = over_y(after(z2b, prior[0]))
    prior = shrink_sums(
        scalars,
        after(tokens, z2b),
        [x1, y1, z2a, x3, y3],
        named(0, [(2, "far"), (3, "own"), (4, "own"), (6, "far"), (7, "own")]),
        prior,
        LIGHT,
    )
    base_fars = [over_cores(after(far, prior[0])) for far in fars]
    prior = shrink_sums(
        scalars,
        tokens,
        [z2b, x1y, x3y, y2a],
        named(0, [(4, "far"), (3, "far"), (7, "far"), (5, "own")]),
        prior,
        HEAVY,
    )
    base = mine + jnp.concatenate(base_fars, axis=0)
    sums, ups = shrink_sums(
        scalars, tokens, [y2b], named(0, [(5, "far")]), prior, LIGHT
    )
    far_sums = over_cores(sums)
    return final_keys(place, block_live_tokens, base, sums, far_sums, ups)


def per_device_gathered(
    tokens,
    key_projection_weight,
    adapter_down_weight,
    adapter_up_weight,
    adapter_pool_index,
    block_adapter_index,
    block_live_tokens,
):
    rows = tokens.shape[0]
    blocks = rows // BLK
    first_block = lax.axis_index("dp") * blocks
    slots = lax.dynamic_slice_in_dim(
        adapter_pool_index[block_adapter_index[:, 0]], first_block, blocks
    )
    fill = lax.dynamic_slice_in_dim(block_live_tokens, first_block, blocks)
    base_part = jnp.dot(tokens, key_projection_weight, preferred_element_type=jnp.float32)
    down = lax.all_gather(adapter_down_weight, "dp", axis=0, tiled=True)
    up = lax.all_gather(adapter_up_weight, "dp", axis=0, tiled=True)
    token_blocks = tokens.reshape(blocks, BLK, tokens.shape[1])
    shrink = jnp.einsum(
        "nrd,nbd->rnb",
        jnp.take(down, slots, axis=0),
        token_blocks,
        preferred_element_type=jnp.float32,
    )
    shrink = lax.psum(shrink.reshape(ADAPTER_RANK, rows), "tensor")
    delta = jnp.einsum(
        "rnb,nrc->nbc",
        shrink.reshape(ADAPTER_RANK, blocks, BLK),
        jnp.take(up, slots, axis=0).astype(jnp.float32),
        precision=lax.Precision.HIGHEST,
        preferred_element_type=jnp.float32,
    )
    base = lax.psum_scatter(base_part, "tensor", scatter_dimension=1, tiled=True)
    mask = jnp.arange(BLK, dtype=jnp.int32)[None, :] < fill[:, None]
    keys = base + delta.reshape(rows, base.shape[1])
    return jnp.where(mask.reshape(rows, 1), keys, 0.0).astype(jnp.bfloat16)


def solution(mesh):
    in_specs = (
        P(("groups", "dp"), "tensor"),
        P("tensor", None),
        P("dp", None, "tensor"),
        P("dp", None, "tensor"),
        P(),
        P("groups", None),
        P("groups"),
    )
    out_specs = P(("groups", "dp"), "tensor")
    planes = dict(mesh.shape) == {"groups": 2, "dp": 8, "tensor": 2}
    return jax.shard_map(
        per_device_planes if planes else per_device_gathered,
        mesh=mesh,
        in_specs=in_specs,
        out_specs=out_specs,
        check_vma=False,
    )
```

```python
import functools

import jax
import jax.numpy as jnp
from jax import lax
from jax.experimental import pallas as pl
from jax.experimental.pallas import tpu as pltpu
from jax.sharding import PartitionSpec as P

ADAPTER_RANK = 64
BLK = 128
FAR_PARTS = 1
SWAP = [(0, 1), (1, 0)]
NT = (((1,), (1,)), ((), ()))
TN = (((0,), (0,)), ((), ()))


def kernel_params(mebibytes):
    return pltpu.CompilerParams(vmem_limit_bytes=mebibytes * 1024 * 1024)


LIGHT = pl.CostEstimate(flops=1, bytes_accessed=1, transcendentals=0)
HEAVY = pl.CostEstimate(flops=30000000000, bytes_accessed=1, transcendentals=0)


def after(array, *others):
    return lax.optimization_barrier((array, *others))[0]


SMEM = pl.BlockSpec(memory_space=pltpu.SMEM)
VMEM = pl.BlockSpec(memory_space=pltpu.VMEM)
ANY = pl.BlockSpec(memory_space=pl.ANY)


def base_kernel(cuts, other, place, tokens, weight, *refs):
    core = 1 - place[2] if other else place[2]
    base_steps(cuts, core, tokens, weight, refs[:-4], refs[-4:])


def base_steps(cuts, core, tokens, weight, outs, scratch):
    tokens_v, weight_v, t_sem, w_sem = scratch
    part, half = outs[0].shape
    columns = pl.ds(pl.multiple_of(core * half, half), half)
    copies = []
    for step, (start, depth) in enumerate(cuts):
        span = pl.ds(start, depth)
        pair = (
            pltpu.make_async_copy(tokens.at[:, span], tokens_v.at[:, span], t_sem.at[step]),
            pltpu.make_async_copy(weight.at[span, columns], weight_v.at[span, :], w_sem.at[step]),
        )
        for copy in pair:
            copy.start()
        copies.append(pair)
    for step, (start, depth) in enumerate(cuts):
        for copy in copies[step]:
            copy.wait()
        for at, out in enumerate(outs):
            product = jnp.dot(
                tokens_v[pl.ds(at * part, part), pl.ds(start, depth)],
                weight_v[pl.ds(start, depth), :],
                preferred_element_type=jnp.float32,
            )
            out[...] = product if step == 0 else out[...] + product


def base_cuts(width):
    eighth = width // 8
    return [(0, eighth)] + [(at * eighth, 2 * eighth) for at in (1, 3, 5)] + [(7 * eighth, eighth)]


def base_scratch(tokens, weight):
    rows, width = tokens.shape
    steps = len(base_cuts(width))
    return [
        pltpu.VMEM((rows, width), tokens.dtype),
        pltpu.VMEM((width, weight.shape[1] // 2), weight.dtype),
        pltpu.SemaphoreType.DMA((steps,)),
        pltpu.SemaphoreType.DMA((steps,)),
    ]


def base_sums(place, tokens, weight, other, parts, hint):
    rows, width = tokens.shape
    half = weight.shape[1] // 2
    return pl.pallas_call(
        functools.partial(base_kernel, base_cuts(width), other),
        in_specs=[SMEM, ANY, ANY],
        out_specs=[VMEM] * parts,
        out_shape=[jax.ShapeDtypeStruct((rows // parts, half), jnp.float32)] * parts,
        scratch_shapes=base_scratch(tokens, weight),
        compiler_params=kernel_params(50),
        cost_estimate=hint,
    )(place, tokens, weight)


def entry_of(place, slot):
    back = ((place[1] >> 1) - (slot >> 1)) & 3
    return 2 * back + ((slot ^ place[1]) & 1)


def side_of(place, kind):
    return {"a": 0, "b": 1, "own": place[0], "far": 1 - place[0]}[kind]


def start_maps(pieces, entry_at, place, arrays, maps_v, up_map, sems, start_tokens):
    m_sem, u_sem = sems
    blocks, _, _, wide = maps_v.shape

    def start(block, carry):
        entry = entry_at(block)
        for at_entry, kind, (at, column), (up_at, up_column), half in pieces:

            @pl.when(entry == at_entry)
            def _(kind=kind, at=at, column=column, up_at=up_at, up_column=up_column):
                side = side_of(place, kind)
                start_tokens(block, side)
                pltpu.make_async_copy(
                    arrays[at].at[:, column : column + wide],
                    maps_v.at[block, side],
                    m_sem.at[block, side],
                ).start()
                pltpu.make_async_copy(
                    arrays[up_at].at[:, up_column : up_column + half],
                    up_map.at[block, :, pl.ds(pl.multiple_of(side * half, half), half)],
                    u_sem.at[block, side],
                ).start()

        return carry

    lax.fori_loop(0, blocks, start, 0)


def add_maps(pieces, entry_at, place, maps_v, tokens_v, up_map, sums, sems, wait_tokens):
    m_sem, u_sem = sems
    blocks, _, _, wide = maps_v.shape
    half = up_map.shape[2] // 2
    masks = []
    for side in range(2):
        bits = {"a": 0, "b": 0, "own": 0, "far": 0}
        for entry, kind, *_ in pieces:
            bits[kind] |= 1 << entry
        masks.append(
            bits["a" if side == 0 else "b"]
            | jnp.where(place[0] == side, bits["own"], bits["far"])
        )

    def add(block, carry):
        entry = entry_at(block)
        for side in range(2):

            @pl.when(((masks[side] >> entry) & 1) == 1)
            def _(side=side):
                wait_tokens(block, side)
                pltpu.make_async_copy(
                    maps_v.at[block, side], maps_v.at[block, side], m_sem.at[block, side]
                ).wait()
                sums[block] += lax.dot_general(
                    maps_v[block, side],
                    tokens_v[pl.ds(pl.multiple_of(block * BLK, BLK), BLK), pl.ds(side * wide, wide)],
                    NT,
                    preferred_element_type=jnp.float32,
                )
                half_map = up_map.at[block, :, pl.ds(side * half, half)]
                pltpu.make_async_copy(half_map, half_map, u_sem.at[block, side]).wait()

        return carry

    lax.fori_loop(0, blocks, add, 0)


def map_scratch(blocks, wide, dtype):
    return [
        pltpu.VMEM((blocks, 2, ADAPTER_RANK, wide), dtype),
        pltpu.SemaphoreType.DMA((blocks, 2)),
        pltpu.SemaphoreType.DMA((blocks, 2)),
    ]


def shrink_kernel(pieces, count, prior_count, place, pool_index, adapter_index, tokens, *refs):
    arrays, priors = refs[:count], refs[count : count + prior_count]
    sums, up_map, tokens_v, t_sem, maps_v, m_sem, u_sem = refs[count + prior_count :]
    blocks, wide = sums.shape[0], maps_v.shape[3]

    def entry_at(block):
        return entry_of(place, pool_index[adapter_index[place[1] * blocks + block]])

    def token_copy(block, side):
        place_of = (
            pl.ds(pl.multiple_of(block * BLK, BLK), BLK),
            pl.ds(pl.multiple_of(side * wide, wide), wide),
        )
        return pltpu.make_async_copy(
            tokens.at[place_of], tokens_v.at[place_of], t_sem.at[block, side]
        )

    start_maps(
        pieces, entry_at, place, arrays, maps_v, up_map, (m_sem, u_sem),
        lambda block, side: token_copy(block, side).start(),
    )
    sums[...] = priors[0][...] if priors else jnp.zeros_like(sums)
    add_maps(
        pieces, entry_at, place, maps_v, tokens_v, up_map, sums, (m_sem, u_sem),
        lambda block, side: token_copy(block, side).wait(),
    )


def shrink_sums(scalars, tokens, arrays, pieces, prior, hint):
    rows, width = tokens.shape
    blocks, count = rows // BLK, len(arrays)
    half = pieces[0][-1]
    return pl.pallas_call(
        functools.partial(shrink_kernel, pieces, count, len(prior)),
        in_specs=[SMEM, SMEM, SMEM] + [ANY] * (1 + count) + [VMEM, ANY][: len(prior)],
        out_specs=[VMEM, ANY],
        out_shape=[
            jax.ShapeDtypeStruct((blocks, ADAPTER_RANK, BLK), jnp.float32),
            jax.ShapeDtypeStruct((blocks, ADAPTER_RANK, 2 * half), jnp.bfloat16),
        ],
        input_output_aliases={5 + count: 1} if prior else {},
        scratch_shapes=[
            pltpu.VMEM((rows, width), tokens.dtype),
            pltpu.SemaphoreType.DMA((blocks, 2)),
        ]
        + map_scratch(blocks, width // 2, tokens.dtype),
        compiler_params=kernel_params(50),
        cost_estimate=hint,
    )(*scalars, tokens, *arrays, *prior)


def final_kernel(place, live, base, sums, far_sums, ups, keys):
    blocks, _, half = ups.shape
    for block in range(blocks):
        total = sums[block] + far_sums[block]
        high = total.astype(jnp.bfloat16)
        rest = total - high.astype(jnp.float32)
        middle = rest.astype(jnp.bfloat16)
        low = (rest - middle.astype(jnp.float32)).astype(jnp.bfloat16)
        up = ups[block]
        delta = lax.dot_general(
            jnp.concatenate([high, middle, low], axis=0),
            jnp.concatenate([up, up, up], axis=0),
            TN,
            preferred_element_type=jnp.float32,
        )
        row = lax.broadcasted_iota(jnp.int32, (BLK, half), 0)
        fill = live[place[1] * blocks + block]
        span = slice(block * BLK, (block + 1) * BLK)
        keys[span, :] = jnp.where(row < fill, base[span, :] + delta, 0.0).astype(keys.dtype)


def final_keys(place, live, base, sums, far_sums, ups):
    rows, half = base.shape
    return pl.pallas_call(
        final_kernel,
        in_specs=[SMEM, SMEM] + [VMEM] * 4,
        out_specs=VMEM,
        out_shape=jax.ShapeDtypeStruct((rows, half), jnp.bfloat16),
        compiler_params=kernel_params(12),
        cost_estimate=LIGHT,
    )(place, live, base, sums, far_sums, ups)


def per_device_planes(
    tokens,
    key_projection_weight,
    adapter_down_weight,
    adapter_up_weight,
    adapter_pool_index,
    block_adapter_index,
    block_live_tokens,
):
    place = jnp.stack(
        [lax.axis_index("groups"), lax.axis_index("dp"), lax.axis_index("tensor")]
    ).astype(jnp.int32)
    down, up = adapter_down_weight[0], adapter_up_weight[0]
    width, half = down.shape[1] // 2, up.shape[1] // 2
    piece = width + half
    own = jnp.concatenate([down, up], axis=1)
    first = lax.axis_index("groups") == 0
    own_ = lax.optimization_barrier(own)
    own_half = jnp.concatenate(
        [
            jnp.where(first, own_[:, :width], own_[:, width : 2 * width]),
            jnp.where(first, own_[:, 2 * width : 2 * width + half], own_[:, 2 * width + half :]),
        ],
        axis=1,
    )

    def ring(array, step):
        pairs = [(2 * z + y, 2 * ((z + step) % 4) + y) for z in range(4) for y in range(2)]
        return lax.ppermute(array, "dp", pairs)

    def over_y(array):
        return lax.ppermute(array, "dp", [(i, i ^ 1) for i in range(8)])

    def over_x(array):
        return lax.ppermute(array, "groups", SWAP)

    def over_cores(array):
        return lax.ppermute(array, "tensor", SWAP)

    scalars = (place, adapter_pool_index, block_adapter_index[:, 0])
    weight = key_projection_weight
    z1 = ring(own_half, 1)
    y0 = over_y(own)
    z3 = ring(own_half, -1)
    fars = base_sums(place, tokens, weight, True, FAR_PARTS, LIGHT)
    z1_ = after(z1, fars[0])
    x1 = over_x(z1_)
    y1 = over_y(z1_)
    z3_ = after(z3, z1_)
    z2a = ring(after(z1_, z3), 1)
    x3 = over_x(z3_)
    y3 = over_y(after(z3_, y0))
    z2b = ring(x1, 1)
    y2a = over_y(after(z2a, y3))
    x1y = over_x(y1)

    (mine,) = base_sums(place, after(tokens, z3_, y0), weight, False, 1, HEAVY)
    def named(first, entries):
        return [
            (entry, kind, (first + at, 0), (first + at, width), half)
            for at, (entry, kind) in enumerate(entries)
        ]

    prior = shrink_sums(
        scalars,
        after(tokens, mine, x1, y1, z2a, y3),
        [down, up, y0, z1, z3],
        [
            (0, "a", (0, 0), (1, 0), half),
            (0, "b", (0, width), (1, half), half),
            (1, "a", (2, 0), (2, 2 * width), half),
            (1, "b", (2, width), (2, 2 * width + half), half),
        ]
        + named(3, [(2, "own"), (6, "own")]),
        [],
        HEAVY,
    )
    x3y = over_x(y3)
    y2b = over_y(after(z2b, prior[0]))
    prior = shrink_sums(
        scalars,
        after(tokens, z2b),
        [x1, y1, z2a, x3, y3],
        named(0, [(2, "far"), (3, "own"), (4, "own"), (6, "far"), (7, "own")]),
        prior,
        LIGHT,
    )
    base_fars = [over_cores(after(far, prior[0])) for far in fars]
    prior = shrink_sums(
        scalars,
        tokens,
        [z2b, x1y, x3y, y2a],
        named(0, [(4, "far"), (3, "far"), (7, "far"), (5, "own")]),
        prior,
        HEAVY,
    )
    base = mine + jnp.concatenate(base_fars, axis=0)
    sums, ups = shrink_sums(
        scalars, tokens, [y2b], named(0, [(5, "far")]), prior, LIGHT
    )
    far_sums = over_cores(sums)
    return final_keys(place, block_live_tokens, base, sums, far_sums, ups)


def per_device_gathered(
    tokens,
    key_projection_weight,
    adapter_down_weight,
    adapter_up_weight,
    adapter_pool_index,
    block_adapter_index,
    block_live_tokens,
):
    rows = tokens.shape[0]
    blocks = rows // BLK
    first_block = lax.axis_index("dp") * blocks
    slots = lax.dynamic_slice_in_dim(
        adapter_pool_index[block_adapter_index[:, 0]], first_block, blocks
    )
    fill = lax.dynamic_slice_in_dim(block_live_tokens, first_block, blocks)
    base_part = jnp.dot(tokens, key_projection_weight, preferred_element_type=jnp.float32)
    down = lax.all_gather(adapter_down_weight, "dp", axis=0, tiled=True)
    up = lax.all_gather(adapter_up_weight, "dp", axis=0, tiled=True)
    token_blocks = tokens.reshape(blocks, BLK, tokens.shape[1])
    shrink = jnp.einsum(
        "nrd,nbd->rnb",
        jnp.take(down, slots, axis=0),
        token_blocks,
        preferred_element_type=jnp.float32,
    )
    shrink = lax.psum(shrink.reshape(ADAPTER_RANK, rows), "tensor")
    delta = jnp.einsum(
        "rnb,nrc->nbc",
        shrink.reshape(ADAPTER_RANK, blocks, BLK),
        jnp.take(up, slots, axis=0).astype(jnp.float32),
        precision=lax.Precision.HIGHEST,
        preferred_element_type=jnp.float32,
    )
    base = lax.psum_scatter(base_part, "tensor", scatter_dimension=1, tiled=True)
    mask = jnp.arange(BLK, dtype=jnp.int32)[None, :] < fill[:, None]
    keys = base + delta.reshape(rows, base.shape[1])
    return jnp.where(mask.reshape(rows, 1), keys, 0.0).astype(jnp.bfloat16)


def solution(mesh):
    in_specs = (
        P(("groups", "dp"), "tensor"),
        P("tensor", None),
        P("dp", None, "tensor"),
        P("dp", None, "tensor"),
        P(),
        P("groups", None),
        P("groups"),
    )
    out_specs = P(("groups", "dp"), "tensor")
    planes = dict(mesh.shape) == {"groups": 2, "dp": 8, "tensor": 2}
    return jax.shard_map(
        per_device_planes if planes else per_device_gathered,
        mesh=mesh,
        in_specs=in_specs,
        out_specs=out_specs,
        check_vma=False,
    )
```
